32 devices in a mesh: ta: 8 (over z, x), gz: 2 (over y), gy: 2 (over core).
Axes of the slice: x: 2, y: 2, z: 4, core: 2. Of those that a mesh axis runs over, the one named last changes fastest.
Arguments:
- source_field: bfloat16 [8, 4, 4, 2, 256, 128], P('ta', 'gz', 'gy'), may hold values from -6 to 6
- clover: bfloat16 [8, 4, 4, 2, 128, 128], P('ta', 'gz', 'gy'), may hold values from -0.1875 to 0.1875
- forward: bfloat16 [4, 8, 4, 4, 2, 128, 128], P(None, 'ta', 'gz', 'gy'), may hold values from -0.1875 to 0.1875
- backward: bfloat16 [4, 8, 4, 4, 2, 128, 128], P(None, 'ta', 'gz', 'gy'), may hold values from -0.1875 to 0.1875
- restrict_blocks: bfloat16 [8, 4, 4, 2, 128, 128], P('ta', 'gz', 'gy'), may hold values from -0.1875 to 0.1875
Outputs:
- second_image: bfloat16 [8, 4, 4, 2, 256, 128], P('ta', 'gz', 'gy')
- restricted: bfloat16 [8, 4, 256, 128], P('ta')
The draws below stay inside these ranges and needn't reach their ends.
All inputs are finite; a program needn't handle non-finite values.
Results may differ from the reference program's by a relative error of at most 0.0064.
Values may be sent and summed in bfloat16 or wider, within the bound.
A program may use at most 64 MiB of HBM per device.

```python
import jax
import jax.numpy as jnp
from jax import lax

NV = 128
NR = 256
LT = 1
LZ = 2
LY = 2
LX = 2
NT = 8
NZ = 4
NY = 4
N_TA = 8
N_GZ = 2
N_GY = 2


def block_levels(stream_key, dims, cuts, least, high):
    loudness, own = 1.0, jax.random.fold_in(stream_key, 6)
    for position, parts in cuts:
        heights = jnp.exp(jax.random.uniform(jax.random.fold_in(own, position), (parts,), jnp.float32, least / len(cuts), high / len(cuts)))
        loudness = loudness * jnp.repeat(heights, dims[position] // parts).reshape([-1 if axis == position else 1 for axis in range(len(dims))])
    return loudness


def noise(stream_key, shape, width, bound, split=(), kind=jnp.bfloat16):
    result = width * jax.random.normal(stream_key, shape, jnp.float32)
    if split:
        result = result * block_levels(stream_key, shape, split, -0.22, 0.18)
    return jnp.clip(result, -bound, bound).astype(kind)


def setup_inputs(seed: int = 0) -> dict:
    key_of = jax.random.split(jax.random.key(seed), 6)
    return {
        "source_field": noise(key_of[0], (NT, NZ, NY, LX, NR, NV), 1.0, 6.0, ((0, 8), (1, 2), (2, 2))),
        "clover": noise(key_of[1], (NT, NZ, NY, LX, NV, NV), (9 * NV) ** -0.5, 0.1875, ((0, 8), (1, 2), (2, 2))),
        "forward": noise(key_of[2], (4, NT, NZ, NY, LX, NV, NV), (9 * NV) ** -0.5, 0.1875, ((1, 8), (2, 2), (3, 2))),
        "backward": noise(key_of[3], (4, NT, NZ, NY, LX, NV, NV), (9 * NV) ** -0.5, 0.1875, ((1, 8), (2, 2), (3, 2))),
        "restrict_blocks": noise(key_of[4], (NT, NZ, NY, LX, NV, NV), (LT * LZ * LY * LX * NV) ** -0.5, 0.1875, ((0, 8), (1, 2), (2, 2))),
    }


def apply_block(blocks, vector):
    return jnp.einsum('tzyxij,tzyxrj->tzyxri', blocks.astype(jnp.float32), vector.astype(jnp.float32))


def operate(vector, clover, forward, backward):
    total = apply_block(clover, vector)
    for axis_id in range(4):
        total = total + apply_block(forward[axis_id], jnp.roll(vector, -1, axis=axis_id))
        formed = lax.optimization_barrier(apply_block(backward[axis_id], vector).astype(jnp.bfloat16))
        total = total + jnp.roll(formed.astype(jnp.float32), 1, axis=axis_id)
    return total.astype(jnp.bfloat16)


def reference(source_field, clover, forward, backward, restrict_blocks):
    first_image = operate(source_field, clover, forward, backward)
    second_image = operate(first_image, clover, forward, backward)
    blocks = restrict_blocks.astype(jnp.float32).reshape(N_TA, LT, N_GZ, LZ, N_GY, LY, LX, NV, NV)
    values = second_image.astype(jnp.float32).reshape(N_TA, LT, N_GZ, LZ, N_GY, LY, LX, NR, NV)
    summed = jnp.einsum('apbqcrxij,apbqcrxkj->abcki', blocks, values)
    restricted = summed.reshape(N_TA, N_GZ * N_GY, NR, NV).astype(jnp.bfloat16)
    return second_image, restricted
```

```python
import functools

import jax
import jax.numpy as jnp
from jax import lax
from jax.experimental import pallas as pl
from jax.experimental.pallas import tpu as pltpu
from jax.sharding import PartitionSpec as P

MESH = pl.DeviceIdType.MESH
LAG = 2


def times(vector, block):
    return lax.dot_general(
        vector, block, (((1,), (1,)), ((), ())), preferred_element_type=jnp.float32
    )


def kernel(
    sizes,
    src, clo, fwd, bwd, res,
    image, gathered,
    V, T, PZ, PY, PX, B0, C, F, B, R, O, total_r, own_r,
    near_send, near_recv, far_send, far_recv, b0_send, b0_recv,
    z_send, z_recv, y_send, y_recv, local, out_sem, g_send, g_recv, g_local,
):
    n_ta, n_gz, n_gy = sizes
    ta, gz, gy = lax.axis_index("ta"), lax.axis_index("gz"), lax.axis_index("gy")
    odd = lax.rem(ta, 2)
    partner = ta + 1 - 2 * odd
    beyond = lax.rem(ta + 2 - 4 * odd + n_ta, n_ta)
    following = lax.rem(ta + 1, n_ta)
    z_up, z_down = lax.rem(gz + 1, n_gz), lax.rem(gz + n_gz - 1, n_gz)
    y_up, y_down = lax.rem(gy + 1, n_gy), lax.rem(gy + n_gy - 1, n_gy)

    fetch = [
        pltpu.make_async_copy(src, V.at[pl.ds(0, 8)], local.at[0]),
        pltpu.make_async_copy(bwd.at[pl.ds(8, 24)], B, local.at[1]),
        pltpu.make_async_copy(fwd, F, local.at[2]),
        pltpu.make_async_copy(clo, C, local.at[3]),
        pltpu.make_async_copy(res, R, local.at[4]),
    ]
    for copy in fetch:
        copy.start()

    others = [(a, b) for a in range(n_gz) for b in range(n_gy) if (a, b) != (0, 0)]

    def other(a, b):
        return lax.rem(gz + a, n_gz), lax.rem(gz * 0 + gy + b, n_gy)

    barrier = pltpu.get_barrier_semaphore()
    for step in (1, 2, n_ta - 1, n_ta - 2):
        pl.semaphore_signal(
            barrier, inc=1, device_id=(lax.rem(ta + step, n_ta), gz, gy), device_id_type=MESH
        )
    for a, b in others:
        oz, oy = other(a, b)
        pl.semaphore_signal(barrier, inc=1, device_id=(ta, oz, oy), device_id_type=MESH)
    pl.semaphore_wait(barrier, 4 + len(others))

    def remote(source, target, send, recv, device):
        return pltpu.make_async_remote_copy(
            src_ref=source, dst_ref=target, send_sem=send, recv_sem=recv,
            device_id=device, device_id_type=MESH,
        )

    def near(u, source):
        img, s = u // 8, lax.rem(u, 8)
        return remote(source, T.at[img, 1 - odd, s], near_send.at[u], near_recv.at[u],
                      (partner, gz, gy))

    def far(u):
        img, s = u // 8, lax.rem(u, 8)
        return remote(T.at[img, odd, s], T.at[img, 1 - odd, s], far_send.at[u], far_recv.at[u],
                      (beyond, gz, gy))

    def block0(s):
        return remote(bwd.at[s], B0.at[s], b0_send.at[s], b0_recv.at[s], (following, gz, gy))

    def z_vector(u, source):
        img, s = u // 8, lax.rem(u, 8)
        return remote(source, V.at[img * 16 + 8 + s], z_send.at[u], z_recv.at[u + 4],
                      (ta, z_down, gy))

    def z_formed(u):
        img, s = u // 8, lax.rem(u, 8)
        return remote(PZ.at[img * 12 + 4 + s], PZ.at[img * 12 + s - 4], z_send.at[u],
                      z_recv.at[u - 4], (ta, z_up, gy))

    def y_vector(u, source):
        img, s = u // 8, lax.rem(u, 8)
        k = 2 * (s // 4) + lax.rem(s, 2)
        return remote(source, V.at[img * 16 + 12 + k], y_send.at[u], y_recv.at[u + 2],
                      (ta, gz, y_down))

    def y_formed(u):
        img, s = u // 8, lax.rem(u, 8)
        k = 2 * (s // 4) + lax.rem(s, 2)
        return remote(PY.at[img * 12 + s], PY.at[img * 12 + 8 + k], y_send.at[u],
                      y_recv.at[u - 2], (ta, gz, y_up))

    def send_vector(u, source):
        s = lax.rem(u, 8)
        near(u, source).start()

        @pl.when(s < 4)
        def _():
            z_vector(u, source).start()

        @pl.when(lax.rem(s // 2, 2) == 0)
        def _():
            y_vector(u, source).start()

    def form(u):
        img, s = u // 8, lax.rem(u, 8)
        vector = V[img * 16 + s]
        PZ[img * 12 + 4 + s] = times(vector, B[s]).astype(jnp.bfloat16)

        @pl.when(s >= 4)
        def _():
            z_formed(u).start()

        PY[img * 12 + s] = times(vector, B[8 + s]).astype(jnp.bfloat16)

        @pl.when(lax.rem(s // 2, 2) == 1)
        def _():
            y_formed(u).start()

        PX[u] = times(vector, B[16 + s]).astype(jnp.bfloat16)

    @pl.loop(0, 8)
    def _(s):
        block0(s).start()
        send_vector(s, src.at[s])

    fetch[0].wait()
    fetch[1].wait()

    @pl.loop(0, 8)
    def _(s):
        form(s)

    for copy in fetch[2:]:
        copy.wait()
    total_r[...] = jnp.zeros_like(total_r)

    def finish(u):
        img, s = u // 8, lax.rem(u, 8)
        z, y, x = s // 4, lax.rem(s // 2, 2), lax.rem(s, 2)
        k = 2 * z + x
        base = img * 16
        y_next = base + (1 - y) * (s + 2) + y * (12 + k)
        y_from = img * 12 + y * (s - 2) + (1 - y) * (8 + k)
        flip = s + 1 - 2 * x

        @pl.when(u < 8)
        def _():
            block0(s).wait_recv()

        total = times(V[base + s], C[s]) + times(V[base + flip], F[24 + s])
        total = total + PX[img * 8 + flip].astype(jnp.float32)
        remote(V.at[base], V.at[base], z_send.at[u], z_recv.at[u], (ta, z_up, gy)).wait_recv()
        total = total + times(V[base + s + 4], F[8 + s])
        total = total + PZ[img * 12 + s].astype(jnp.float32)
        remote(V.at[base], V.at[base], y_send.at[u], y_recv.at[u], (ta, gz, y_up)).wait_recv()
        total = total + times(V[y_next], F[16 + s])
        total = total + PY[y_from].astype(jnp.float32)
        far(u).wait_recv()
        total = total + times(T[img, 0, s], F[s])
        total = total + times(T[img, 1, s], B0[s]).astype(jnp.bfloat16).astype(jnp.float32)
        value = total.astype(jnp.bfloat16)

        @pl.when(u < 8)
        def _():
            V[16 + s] = value
            send_vector(u + 8, V.at[16 + s])
            form(u + 8)

        @pl.when(u >= 8)
        def _():
            O[s] = value
            pltpu.make_async_copy(O.at[s], image.at[s], out_sem.at[s]).start()
            total_r[...] += times(value, R[s])

    @pl.loop(0, 16 + LAG)
    def _(u):
        @pl.when(u < 16)
        def _():
            near(u, V.at[0]).wait_recv()
            far(u).start()

        @pl.when(u >= LAG)
        def _():
            finish(u - LAG)

    own_r[...] = total_r[...].astype(jnp.bfloat16)
    place = gz * n_gy + gy
    sends = []
    for index, (a, b) in enumerate(others):
        oz, oy = other(a, b)
        copy = remote(own_r, gathered.at[place], g_send.at[index], g_recv.at[index], (ta, oz, oy))
        copy.start()
        sends.append(copy)
    keep = pltpu.make_async_copy(own_r, gathered.at[place], g_local)
    keep.start()

    @pl.loop(0, 16)
    def _(u):
        near(u, V.at[0]).wait_send()
        far(u).wait_send()
        remote(V.at[0], V.at[0], z_send.at[u], z_recv.at[u], (ta, z_up, gy)).wait_send()
        remote(V.at[0], V.at[0], y_send.at[u], y_recv.at[u], (ta, gz, y_up)).wait_send()

    @pl.loop(0, 8)
    def _(s):
        block0(s).wait_send()
        pltpu.make_async_copy(O.at[s], image.at[s], out_sem.at[s]).wait()

    keep.wait()
    for copy in sends:
        copy.wait()


def per_device(sizes, source_field, clover, forward, backward, restrict_blocks):
    n_ta, n_gz, n_gy = sizes
    rows, width = source_field.shape[-2:]
    field = (rows, width)
    block = (width, width)
    others = n_gz * n_gy - 1
    bf16 = jnp.bfloat16
    dma = pltpu.SemaphoreType.DMA
    image, gathered = pl.pallas_call(
        functools.partial(kernel, sizes),
        out_shape=(
            jax.ShapeDtypeStruct((8,) + field, bf16),
            jax.ShapeDtypeStruct((n_gz * n_gy,) + field, bf16),
        ),
        in_specs=[pl.BlockSpec(memory_space=pl.ANY)] * 5,
        out_specs=(pl.BlockSpec(memory_space=pl.ANY), pl.BlockSpec(memory_space=pl.ANY)),
        scratch_shapes=[
            pltpu.VMEM((32,) + field, bf16),
            pltpu.VMEM((2, 2, 8) + field, bf16),
            pltpu.VMEM((24,) + field, bf16),
            pltpu.VMEM((24,) + field, bf16),
            pltpu.VMEM((16,) + field, bf16),
            pltpu.VMEM((8,) + block, bf16),
            pltpu.VMEM((8,) + block, bf16),
            pltpu.VMEM((32,) + block, bf16),
            pltpu.VMEM((24,) + block, bf16),
            pltpu.VMEM((8,) + block, bf16),
            pltpu.VMEM((8,) + field, bf16),
            pltpu.VMEM(field, jnp.float32),
            pltpu.VMEM(field, bf16),
            dma((16,)), dma((16,)), dma((16,)), dma((16,)),
            dma((8,)), dma((8,)),
            dma((16,)), dma((16,)), dma((16,)), dma((16,)),
            dma((5,)), dma((8,)), dma((others,)), dma((others,)), dma,
        ],
        compiler_params=pltpu.CompilerParams(
            collective_id=0, has_side_effects=True, vmem_limit_bytes=40 * 1024 * 1024
        ),
    )(
        source_field.reshape((8,) + field),
        clover.reshape((8,) + block),
        forward.reshape((32,) + block),
        backward.reshape((32,) + block),
        restrict_blocks.reshape((8,) + block),
    )
    return image.reshape(source_field.shape), gathered.reshape((1, n_gz * n_gy) + field)


def solution(mesh):
    sizes = tuple(mesh.shape[axis] for axis in ("ta", "gz", "gy"))
    assert sizes[0] % 2 == 0 and sizes[0] >= 4
    return jax.shard_map(
        functools.partial(per_device, sizes),
        mesh=mesh,
        in_specs=(
            P("ta", "gz", "gy", None, None, None),
            P("ta", "gz", "gy", None, None, None),
            P(None, "ta", "gz", "gy", None, None, None),
            P(None, "ta", "gz", "gy", None, None, None),
            P("ta", "gz", "gy", None, None, None),
        ),
        out_specs=(P("ta", "gz", "gy", None, None, None), P("ta", None, None, None)),
        check_vma=False,
    )
```

```python
import functools

import jax
import jax.numpy as jnp
from jax import lax
from jax.experimental import pallas as pl
from jax.experimental.pallas import tpu as pltpu
from jax.sharding import PartitionSpec as P

MESH = pl.DeviceIdType.MESH
LAG = 2
AHEAD = 3


def times(vector, block):
    return lax.dot_general(
        vector, block, (((1,), (1,)), ((), ())), preferred_element_type=jnp.float32
    )


def kernel(
    sizes,
    src, clo, fwd, bwd, res,
    image, gathered,
    V, T, PZ, PY, PX, B0, C, F, B, R, O, total_r, own_r,
    near_send, near_recv, far_send, far_recv, b0_send, b0_recv,
    z_send, z_recv, y_send, y_recv, local, out_sem, g_send, g_recv, g_local,
):
    n_ta, n_gz, n_gy = sizes
    ta, gz, gy = lax.axis_index("ta"), lax.axis_index("gz"), lax.axis_index("gy")
    odd = lax.rem(ta, 2)
    partner = ta + 1 - 2 * odd
    beyond = lax.rem(ta + 2 - 4 * odd + n_ta, n_ta)
    following = lax.rem(ta + 1, n_ta)
    z_up, z_down = lax.rem(gz + 1, n_gz), lax.rem(gz + n_gz - 1, n_gz)
    y_up, y_down = lax.rem(gy + 1, n_gy), lax.rem(gy + n_gy - 1, n_gy)

    fetch = [
        pltpu.make_async_copy(src, V.at[pl.ds(0, 8)], local.at[0]),
        pltpu.make_async_copy(bwd.at[pl.ds(8, 24)], B, local.at[1]),
        pltpu.make_async_copy(fwd, F, local.at[2]),
        pltpu.make_async_copy(clo, C, local.at[3]),
        pltpu.make_async_copy(res, R, local.at[4]),
    ]
    for copy in fetch:
        copy.start()

    others = [(a, b) for a in range(n_gz) for b in range(n_gy) if (a, b) != (0, 0)]

    def other(a, b):
        return lax.rem(gz + a, n_gz), lax.rem(gz * 0 + gy + b, n_gy)

    barrier = pltpu.get_barrier_semaphore()
    for step in (1, 2, n_ta - 1, n_ta - 2):
        pl.semaphore_signal(
            barrier, inc=1, device_id=(lax.rem(ta + step, n_ta), gz, gy), device_id_type=MESH
        )
    for a, b in others:
        oz, oy = other(a, b)
        pl.semaphore_signal(barrier, inc=1, device_id=(ta, oz, oy), device_id_type=MESH)
    pl.semaphore_wait(barrier, 4 + len(others))

    def remote(source, target, send, recv, device):
        return pltpu.make_async_remote_copy(
            src_ref=source, dst_ref=target, send_sem=send, recv_sem=recv,
            device_id=device, device_id_type=MESH,
        )

    def near(u, source):
        img, s = u // 8, lax.rem(u, 8)
        return remote(source, T.at[img, 1 - odd, s], near_send.at[u], near_recv.at[u],
                      (partner, gz, gy))

    def far(u):
        img, s = u // 8, lax.rem(u, 8)
        return remote(T.at[img, odd, s], T.at[img, 1 - odd, s], far_send.at[u], far_recv.at[u],
                      (beyond, gz, gy))

    def block0(s):
        return remote(bwd.at[s], B0.at[s], b0_send.at[s], b0_recv.at[s], (following, gz, gy))

    def z_vector(u, source):
        img, s = u // 8, lax.rem(u, 8)
        return remote(source, V.at[img * 16 + 8 + s], z_send.at[u], z_recv.at[u + 4],
                      (ta, z_down, gy))

    def z_formed(u):
        img, s = u // 8, lax.rem(u, 8)
        return remote(PZ.at[img * 12 + 4 + s], PZ.at[img * 12 + s - 4], z_send.at[u],
                      z_recv.at[u - 4], (ta, z_up, gy))

    def y_vector(u, source):
        img, s = u // 8, lax.rem(u, 8)
        k = 2 * (s // 4) + lax.rem(s, 2)
        return remote(source, V.at[img * 16 + 12 + k], y_send.at[u], y_recv.at[u + 2],
                      (ta, gz, y_down))

    def y_formed(u):
        img, s = u // 8, lax.rem(u, 8)
        k = 2 * (s // 4) + lax.rem(s, 2)
        return remote(PY.at[img * 12 + s], PY.at[img * 12 + 8 + k], y_send.at[u],
                      y_recv.at[u - 2], (ta, gz, y_up))

    def send_time(u, source):
        near(u, source).start()

        @pl.when(u < 8)
        def _():
            block0(lax.rem(u, 8)).start()

    def send_z(target):
        img, d = target // 8, lax.rem(target, 8)

        @pl.when(d < 4)
        def _():
            z_formed(target + 4).start()

        @pl.when(d >= 4)
        def _():
            z_vector(target - 4, V.at[img * 16 + d - 4]).start()

    def send_vector(u, source):
        s = lax.rem(u, 8)

        @pl.when(lax.rem(s // 2, 2) == 0)
        def _():
            y_vector(u, source).start()

    def form(u):
        img, s = u // 8, lax.rem(u, 8)
        vector = V[img * 16 + s]
        PZ[img * 12 + 4 + s] = times(vector, B[s]).astype(jnp.bfloat16)
        PY[img * 12 + s] = times(vector, B[8 + s]).astype(jnp.bfloat16)

        @pl.when(lax.rem(s // 2, 2) == 1)
        def _():
            y_formed(u).start()

        PX[u] = times(vector, B[16 + s]).astype(jnp.bfloat16)

    @pl.loop(0, 8)
    def _(s):
        @pl.when(s < AHEAD)
        def _():
            send_time(s, src.at[s])

        send_vector(s, src.at[s])

    fetch[0].wait()
    fetch[1].wait()

    @pl.loop(0, 8)
    def _(s):
        form(lax.rem(s + 4, 8))

        @pl.when(s < 4)
        def _():
            send_z(s)

    for copy in fetch[2:]:
        copy.wait()
    total_r[...] = jnp.zeros_like(total_r)

    def finish(u):
        img, s = u // 8, lax.rem(u, 8)
        z, y, x = s // 4, lax.rem(s // 2, 2), lax.rem(s, 2)
        k = 2 * z + x
        base = img * 16
        y_next = base + (1 - y) * (s + 2) + y * (12 + k)
        y_from = img * 12 + y * (s - 2) + (1 - y) * (8 + k)
        flip = s + 1 - 2 * x

        @pl.when(u < 8)
        def _():
            block0(s).wait_recv()

        total = times(V[base + s], C[s]) + times(V[base + flip], F[24 + s])
        total = total + PX[img * 8 + flip].astype(jnp.float32)
        remote(V.at[base], V.at[base], z_send.at[u], z_recv.at[u], (ta, z_up, gy)).wait_recv()
        total = total + times(V[base + s + 4], F[8 + s])
        total = total + PZ[img * 12 + s].astype(jnp.float32)
        remote(V.at[base], V.at[base], y_send.at[u], y_recv.at[u], (ta, gz, y_up)).wait_recv()
        total = total + times(V[y_next], F[16 + s])
        total = total + PY[y_from].astype(jnp.float32)
        far(u).wait_recv()
        total = total + times(T[img, 0, s], F[s])
        total = total + times(T[img, 1, s], B0[s]).astype(jnp.bfloat16).astype(jnp.float32)
        value = total.astype(jnp.bfloat16)

        @pl.when(u < 8)
        def _():
            V[16 + s] = value
            send_vector(u + 8, V.at[16 + s])
            form(u + 8)

        @pl.when(u >= 8)
        def _():
            O[s] = value
            pltpu.make_async_copy(O.at[s], image.at[s], out_sem.at[s]).start()
            total_r[...] += times(value, R[s])

        @pl.when(u < 12)
        def _():
            send_z(u + 4)

    @pl.loop(0, 16 + LAG)
    def _(u):
        @pl.when(u < 16)
        def _():
            near(u, V.at[0]).wait_recv()
            far(u).start()

        @pl.when(u + AHEAD < 16)
        def _():
            v = u + AHEAD
            send_time(v, V.at[v // 8 * 16 + lax.rem(v, 8)])

        @pl.when(u >= LAG)
        def _():
            finish(u - LAG)

    own_r[...] = total_r[...].astype(jnp.bfloat16)
    place = gz * n_gy + gy
    sends = []
    for index, (a, b) in enumerate(others):
        oz, oy = other(a, b)
        copy = remote(own_r, gathered.at[place], g_send.at[index], g_recv.at[index], (ta, oz, oy))
        copy.start()
        sends.append(copy)
    keep = pltpu.make_async_copy(own_r, gathered.at[place], g_local)
    keep.start()

    @pl.loop(0, 16)
    def _(u):
        near(u, V.at[0]).wait_send()
        far(u).wait_send()
        remote(V.at[0], V.at[0], z_send.at[u], z_recv.at[u], (ta, z_up, gy)).wait_send()
        remote(V.at[0], V.at[0], y_send.at[u], y_recv.at[u], (ta, gz, y_up)).wait_send()

    @pl.loop(0, 8)
    def _(s):
        block0(s).wait_send()
        pltpu.make_async_copy(O.at[s], image.at[s], out_sem.at[s]).wait()

    keep.wait()
    for copy in sends:
        copy.wait()


def per_device(sizes, source_field, clover, forward, backward, restrict_blocks):
    n_ta, n_gz, n_gy = sizes
    rows, width = source_field.shape[-2:]
    field = (rows, width)
    block = (width, width)
    others = n_gz * n_gy - 1
    bf16 = jnp.bfloat16
    dma = pltpu.SemaphoreType.DMA
    image, gathered = pl.pallas_call(
        functools.partial(kernel, sizes),
        out_shape=(
            jax.ShapeDtypeStruct((8,) + field, bf16),
            jax.ShapeDtypeStruct((n_gz * n_gy,) + field, bf16),
        ),
        in_specs=[pl.BlockSpec(memory_space=pltpu.HBM)] * 5,
        out_specs=(pl.BlockSpec(memory_space=pltpu.HBM), pl.BlockSpec(memory_space=pltpu.HBM)),
        scratch_shapes=[
            pltpu.VMEM((32,) + field, bf16),
            pltpu.VMEM((2, 2, 8) + field, bf16),
            pltpu.VMEM((24,) + field, bf16),
            pltpu.VMEM((24,) + field, bf16),
            pltpu.VMEM((16,) + field, bf16),
            pltpu.VMEM((8,) + block, bf16),
            pltpu.VMEM((8,) + block, bf16),
            pltpu.VMEM((32,) + block, bf16),
            pltpu.VMEM((24,) + block, bf16),
            pltpu.VMEM((8,) + block, bf16),
            pltpu.VMEM((8,) + field, bf16),
            pltpu.VMEM(field, jnp.float32),
            pltpu.VMEM(field, bf16),
            dma((16,)), dma((16,)), dma((16,)), dma((16,)),
            dma((8,)), dma((8,)),
            dma((16,)), dma((16,)), dma((16,)), dma((16,)),
            dma((5,)), dma((8,)), dma((others,)), dma((others,)), dma,
        ],
        compiler_params=pltpu.CompilerParams(
            collective_id=0, has_side_effects=True, vmem_limit_bytes=60 * 1024 * 1024
        ),
    )(
        source_field.reshape((8,) + field),
        clover.reshape((8,) + block),
        forward.reshape((32,) + block),
        backward.reshape((32,) + block),
        restrict_blocks.reshape((8,) + block),
    )
    return image.reshape(source_field.shape), gathered.reshape((1, n_gz * n_gy) + field)


def solution(mesh):
    sizes = tuple(mesh.shape[axis] for axis in ("ta", "gz", "gy"))
    assert sizes[0] % 2 == 0 and sizes[0] >= 4
    return jax.shard_map(
        functools.partial(per_device, sizes),
        mesh=mesh,
        in_specs=(
            P("ta", "gz", "gy", None, None, None),
            P("ta", "gz", "gy", None, None, None),
            P(None, "ta", "gz", "gy", None, None, None),
            P(None, "ta", "gz", "gy", None, None, None),
            P("ta", "gz", "gy", None, None, None),
        ),
        out_specs=(P("ta", "gz", "gy", None, None, None), P("ta", None, None, None)),
        check_vma=False,
    )
```

```python
import functools

import jax
import jax.numpy as jnp
from jax import lax
from jax.experimental import pallas as pl
from jax.experimental.pallas import tpu as pltpu
from jax.sharding import PartitionSpec as P

MESH = pl.DeviceIdType.MESH
LAG = 5
AHEAD = 6
Z_AHEAD = 8
PARTS = 2
IMAGE = 8 * PARTS
UNITS = 2 * IMAGE


def times(vector, block):
    return lax.dot_general(
        vector, block, (((1,), (1,)), ((), ())), preferred_element_type=jnp.float32
    )


def kernel(
    sizes,
    src, clo, fwd, bwd, res,
    image, gathered,
    V, T, PZ, PY, PX, B0, C, F, B, R, O, total_r, own_r,
    near_send, near_recv, far_send, far_recv, b0_send, b0_recv,
    z_send, z_recv, y_send, y_recv, local, out_sem, g_send, g_recv, g_local,
):
    n_ta, n_gz, n_gy = sizes
    ta, gz, gy = lax.axis_index("ta"), lax.axis_index("gz"), lax.axis_index("gy")
    odd = lax.rem(ta, 2)
    partner = ta + 1 - 2 * odd
    beyond = lax.rem(ta + 2 - 4 * odd + n_ta, n_ta)
    following = lax.rem(ta + 1, n_ta)
    z_up, z_down = lax.rem(gz + 1, n_gz), lax.rem(gz + n_gz - 1, n_gz)
    y_up, y_down = lax.rem(gy + 1, n_gy), lax.rem(gy + n_gy - 1, n_gy)

    fetch = [
        pltpu.make_async_copy(src, V.at[pl.ds(0, 8)], local.at[0]),
        pltpu.make_async_copy(bwd.at[pl.ds(8, 24)], B, local.at[1]),
        pltpu.make_async_copy(fwd, F, local.at[2]),
        pltpu.make_async_copy(clo, C, local.at[3]),
        pltpu.make_async_copy(res, R, local.at[4]),
    ]
    for copy in fetch:
        copy.start()

    others = [(a, b) for a in range(n_gz) for b in range(n_gy) if (a, b) != (0, 0)]

    def other(a, b):
        return lax.rem(gz + a, n_gz), lax.rem(gz * 0 + gy + b, n_gy)

    barrier = pltpu.get_barrier_semaphore()
    for step in (1, 2, n_ta - 1, n_ta - 2):
        pl.semaphore_signal(
            barrier, inc=1, device_id=(lax.rem(ta + step, n_ta), gz, gy), device_id_type=MESH
        )
    for a, b in others:
        oz, oy = other(a, b)
        pl.semaphore_signal(barrier, inc=1, device_id=(ta, oz, oy), device_id_type=MESH)
    pl.semaphore_wait(barrier, 4 + len(others))

    def remote(source, target, send, recv, device):
        return pltpu.make_async_remote_copy(
            src_ref=source, dst_ref=target, send_sem=send, recv_sem=recv,
            device_id=device, device_id_type=MESH,
        )

    rows = src.shape[1] // PARTS

    def split(u):
        part = lax.rem(u // 8, PARTS)
        return u // IMAGE, pl.ds(pl.multiple_of(part * rows, rows), rows), lax.rem(u, 8)

    def near(u, source):
        img, r, s = split(u)
        return remote(source.at[r], T.at[img, 1 - odd, s, r], near_send.at[u], near_recv.at[u],
                      (partner, gz, gy))

    def far(u):
        img, r, s = split(u)
        return remote(T.at[img, odd, s, r], T.at[img, 1 - odd, s, r], far_send.at[u],
                      far_recv.at[u], (beyond, gz, gy))

    def block0(s):
        return remote(bwd.at[s], B0.at[s], b0_send.at[s], b0_recv.at[s], (following, gz, gy))

    def z_vector(u):
        img, r, s = split(u)
        return remote(V.at[img * 16 + s, r], V.at[img * 16 + 8 + s, r], z_send.at[u],
                      z_recv.at[u + 4], (ta, z_down, gy))

    def z_formed(u):
        img, r, s = split(u)
        return remote(PZ.at[img * 12 + 4 + s, r], PZ.at[img * 12 + s - 4, r], z_send.at[u],
                      z_recv.at[u - 4], (ta, z_up, gy))

    def z_any(u):
        return remote(V.at[0, pl.ds(0, rows)], V.at[0, pl.ds(0, rows)], z_send.at[u],
                      z_recv.at[u], (ta, z_up, gy))

    def y_vector(u):
        img, r, s = split(u)
        k = 2 * (s // 4) + lax.rem(s, 2)
        return remote(V.at[img * 16 + s, r], V.at[img * 16 + 12 + k, r], y_send.at[u],
                      y_recv.at[u + 2], (ta, gz, y_down))

    def y_formed(u):
        img, r, s = split(u)
        k = 2 * (s // 4) + lax.rem(s, 2)
        return remote(PY.at[img * 12 + s, r], PY.at[img * 12 + 8 + k, r], y_send.at[u],
                      y_recv.at[u - 2], (ta, gz, y_up))

    def y_any(u):
        return remote(V.at[0, pl.ds(0, rows)], V.at[0, pl.ds(0, rows)], y_send.at[u],
                      y_recv.at[u], (ta, gz, y_up))

    def send_time(u, source):
        near(u, source).start()

        @pl.when(u < 8)
        def _():
            block0(lax.rem(u, 8)).start()

    def send_z(target):
        @pl.when(lax.rem(target, 8) < 4)
        def _():
            z_formed(target + 4).start()

        @pl.when(lax.rem(target, 8) >= 4)
        def _():
            z_vector(target - 4).start()

    def send_y(u):
        y = lax.rem(u // 2, 2)

        @pl.when(y == 0)
        def _():
            y_vector(u).start()

        @pl.when(y == 1)
        def _():
            y_formed(u).start()

    def form(img, r, s, vector):
        block = jnp.concatenate([B[s], B[8 + s], B[16 + s]], axis=0)
        formed = times(vector, block).astype(jnp.bfloat16)
        width = vector.shape[1]
        PZ[img * 12 + 4 + s, r] = formed[:, :width]
        PY[img * 12 + s, r] = formed[:, width : 2 * width]
        PX[img * 8 + s, r] = formed[:, 2 * width :]

    @pl.loop(0, AHEAD)
    def _(u):
        send_time(u, src.at[lax.rem(u, 8)])

    fetch[0].wait()
    fetch[1].wait()

    @pl.loop(0, 8)
    def _(index):
        s = lax.rem(index + 4, 8)
        everything = pl.ds(0, PARTS * rows)
        form(0, everything, s, V[s])

        @pl.when(index < 4)
        def _():
            send_z(index)

        send_y(s)

    @pl.loop(4, Z_AHEAD)
    def _(u):
        send_z(u)

    @pl.loop(8, IMAGE)
    def _(u):
        send_y(u)

    for copy in fetch[2:]:
        copy.wait()
    total_r[...] = jnp.zeros_like(total_r)

    place = gz * n_gy + gy

    def gather(part):
        r = pl.ds(pl.multiple_of(part * rows, rows), rows)
        copies = [pltpu.make_async_copy(own_r.at[r], gathered.at[place, r], g_local.at[part])]
        for index, (a, b) in enumerate(others):
            oz, oy = other(a, b)
            copies.append(remote(own_r.at[r], gathered.at[place, r], g_send.at[part, index],
                                 g_recv.at[part, index], (ta, oz, oy)))
        return copies

    def result(u):
        img, r, s = split(u)
        return pltpu.make_async_copy(O.at[s, r], image.at[s, r], out_sem.at[u - IMAGE])

    def finish(u):
        img, r, s = split(u)
        z, y, x = s // 4, lax.rem(s // 2, 2), lax.rem(s, 2)
        k = 2 * z + x
        base = img * 16
        y_next = base + (1 - y) * (s + 2) + y * (12 + k)
        y_from = img * 12 + y * (s - 2) + (1 - y) * (8 + k)
        flip = s + 1 - 2 * x

        @pl.when(u < 8)
        def _():
            block0(s).wait_recv()

        z_any(u).wait_recv()
        y_any(u).wait_recv()
        far(u).wait_recv()
        vectors = [V[base + s, r], V[base + flip, r], V[base + s + 4, r], V[y_next, r],
                   T[img, 0, s, r]]
        blocks = [C[s], F[24 + s], F[8 + s], F[16 + s], F[s]]
        total = times(jnp.concatenate(vectors, axis=1), jnp.concatenate(blocks, axis=1))
        for formed in (PX[img * 8 + flip, r], PZ[img * 12 + s, r], PY[y_from, r],
                       times(T[img, 1, s, r], B0[s]).astype(jnp.bfloat16)):
            total = total + formed.astype(jnp.float32)
        value = total.astype(jnp.bfloat16)

        @pl.when(u < IMAGE)
        def _():
            V[16 + s, r] = value
            form(1, r, s, value)
            send_y(u + IMAGE)

        @pl.when(u >= IMAGE)
        def _():
            O[s, r] = value
            result(u).start()
            total_r[r] += times(value, R[s])

            @pl.when(s == 7)
            def _():
                own_r[r] = total_r[r].astype(jnp.bfloat16)
                for copy in gather(lax.rem(u // 8, PARTS)):
                    copy.start()

        @pl.when(u + Z_AHEAD < UNITS)
        def _():
            send_z(u + Z_AHEAD)

    @pl.loop(0, UNITS + LAG)
    def _(u):
        @pl.when(u < UNITS)
        def _():
            near(u, V.at[0]).wait_recv()
            far(u).start()

        @pl.when(u + AHEAD < UNITS)
        def _():
            v = u + AHEAD
            send_time(v, V.at[v // IMAGE * 16 + lax.rem(v, 8)])

        @pl.when(u >= LAG)
        def _():
            finish(u - LAG)

    @pl.loop(0, UNITS)
    def _(u):
        near(u, V.at[0]).wait_send()
        far(u).wait_send()
        z_any(u).wait_send()
        y_any(u).wait_send()

    @pl.loop(0, 8)
    def _(s):
        block0(s).wait_send()

    @pl.loop(IMAGE, UNITS)
    def _(u):
        result(u).wait()

    @pl.loop(0, PARTS)
    def _(part):
        for copy in gather(part):
            copy.wait()


def per_device(sizes, source_field, clover, forward, backward, restrict_blocks):
    n_ta, n_gz, n_gy = sizes
    rows, width = source_field.shape[-2:]
    field = (rows, width)
    block = (width, width)
    others = n_gz * n_gy - 1
    bf16 = jnp.bfloat16
    dma = pltpu.SemaphoreType.DMA
    image, gathered = pl.pallas_call(
        functools.partial(kernel, sizes),
        out_shape=(
            jax.ShapeDtypeStruct((8,) + field, bf16),
            jax.ShapeDtypeStruct((n_gz * n_gy,) + field, bf16),
        ),
        in_specs=[pl.BlockSpec(memory_space=pltpu.HBM)] * 5,
        out_specs=(pl.BlockSpec(memory_space=pltpu.HBM), pl.BlockSpec(memory_space=pltpu.HBM)),
        scratch_shapes=[
            pltpu.VMEM((32,) + field, bf16),
            pltpu.VMEM((2, 2, 8) + field, bf16),
            pltpu.VMEM((24,) + field, bf16),
            pltpu.VMEM((24,) + field, bf16),
            pltpu.VMEM((16,) + field, bf16),
            pltpu.VMEM((8,) + block, bf16),
            pltpu.VMEM((8,) + block, bf16),
            pltpu.VMEM((32,) + block, bf16),
            pltpu.VMEM((24,) + block, bf16),
            pltpu.VMEM((8,) + block, bf16),
            pltpu.VMEM((8,) + field, bf16),
            pltpu.VMEM(field, jnp.float32),
            pltpu.VMEM(field, bf16),
            dma((UNITS,)), dma((UNITS,)), dma((UNITS,)), dma((UNITS,)),
            dma((8,)), dma((8,)),
            dma((UNITS,)), dma((UNITS,)), dma((UNITS,)), dma((UNITS,)),
            dma((5,)), dma((IMAGE,)), dma((PARTS, others)), dma((PARTS, others)), dma((PARTS,)),
        ],
        compiler_params=pltpu.CompilerParams(
            collective_id=0, has_side_effects=True, vmem_limit_bytes=60 * 1024 * 1024
        ),
    )(
        source_field.reshape((8,) + field),
        clover.reshape((8,) + block),
        forward.reshape((32,) + block),
        backward.reshape((32,) + block),
        restrict_blocks.reshape((8,) + block),
    )
    return image.reshape(source_field.shape), gathered.reshape((1, n_gz * n_gy) + field)


def solution(mesh):
    sizes = tuple(mesh.shape[axis] for axis in ("ta", "gz", "gy"))
    assert sizes[0] % 2 == 0 and sizes[0] >= 4
    return jax.shard_map(
        functools.partial(per_device, sizes),
        mesh=mesh,
        in_specs=(
            P("ta", "gz", "gy", None, None, None),
            P("ta", "gz", "gy", None, None, None),
            P(None, "ta", "gz", "gy", None, None, None),
            P(None, "ta", "gz", "gy", None, None, None),
            P("ta", "gz", "gy", None, None, None),
        ),
        out_specs=(P("ta", "gz", "gy", None, None, None), P("ta", None, None, None)),
        check_vma=False,
    )
```

```python
import functools

import jax
import jax.numpy as jnp
from jax import lax
from jax.experimental import pallas as pl
from jax.experimental.pallas import tpu as pltpu
from jax.sharding import PartitionSpec as P

MESH = pl.DeviceIdType.MESH
LAG = 4
AHEAD = 6
Z_AHEAD = 8
PARTS = 2
IMAGE = 8 * PARTS
UNITS = 2 * IMAGE


def times(vector, block):
    return lax.dot_general(
        vector, block, (((1,), (1,)), ((), ())), preferred_element_type=jnp.float32
    )


def kernel(
    sizes,
    src, clo, fwd, bwd, res,
    image, gathered,
    V, T, PZ, PY, PX, TB, C, F, B, R, O, early, total_r, own_r,
    near_send, near_recv, far_send, far_recv, b0_send, b0_recv,
    z_send, z_recv, y_send, y_recv, local, out_sem, g_send, g_recv, g_local,
):
    n_ta, n_gz, n_gy = sizes
    ta, gz, gy = lax.axis_index("ta"), lax.axis_index("gz"), lax.axis_index("gy")
    odd = lax.rem(ta, 2)
    partner = ta + 1 - 2 * odd
    beyond = lax.rem(ta + 2 - 4 * odd + n_ta, n_ta)
    following = lax.rem(ta + 1, n_ta)
    z_up, z_down = lax.rem(gz + 1, n_gz), lax.rem(gz + n_gz - 1, n_gz)
    y_up, y_down = lax.rem(gy + 1, n_gy), lax.rem(gy + n_gy - 1, n_gy)

    fetch = [
        pltpu.make_async_copy(src, V.at[pl.ds(0, 8)], local.at[0]),
        pltpu.make_async_copy(bwd.at[pl.ds(8, 24)], B, local.at[1]),
        pltpu.make_async_copy(fwd.at[pl.ds(8, 24)], F, local.at[2]),
        pltpu.make_async_copy(clo, C, local.at[3]),
        pltpu.make_async_copy(res, R, local.at[4]),
        pltpu.make_async_copy(fwd.at[pl.ds(0, 8)], TB.at[0], local.at[5]),
    ]
    for copy in fetch:
        copy.start()

    others = [(a, b) for a in range(n_gz) for b in range(n_gy) if (a, b) != (0, 0)]

    def other(a, b):
        return lax.rem(gz + a, n_gz), lax.rem(gz * 0 + gy + b, n_gy)

    barrier = pltpu.get_barrier_semaphore()
    for step in (1, 2, n_ta - 1, n_ta - 2):
        pl.semaphore_signal(
            barrier, inc=1, device_id=(lax.rem(ta + step, n_ta), gz, gy), device_id_type=MESH
        )
    for a, b in others:
        oz, oy = other(a, b)
        pl.semaphore_signal(barrier, inc=1, device_id=(ta, oz, oy), device_id_type=MESH)
    pl.semaphore_wait(barrier, 4 + len(others))

    def remote(source, target, send, recv, device):
        return pltpu.make_async_remote_copy(
            src_ref=source, dst_ref=target, send_sem=send, recv_sem=recv,
            device_id=device, device_id_type=MESH,
        )

    rows = src.shape[1] // PARTS

    def split(u):
        part = lax.rem(u // 8, PARTS)
        return u // IMAGE, pl.ds(pl.multiple_of(part * rows, rows), rows), lax.rem(u, 8)

    def near(u, source):
        img, r, s = split(u)
        return remote(source.at[r], T.at[img, 1 - odd, s, r], near_send.at[u], near_recv.at[u],
                      (partner, gz, gy))

    def far(u):
        img, r, s = split(u)
        return remote(T.at[img, odd, s, r], T.at[img, 1 - odd, s, r], far_send.at[u],
                      far_recv.at[u], (beyond, gz, gy))

    def block0(s):
        return remote(bwd.at[s], TB.at[1, s], b0_send.at[s], b0_recv.at[s], (following, gz, gy))

    def z_vector(u):
        img, r, s = split(u)
        return remote(V.at[img * 16 + s, r], V.at[img * 16 + 8 + s, r], z_send.at[u],
                      z_recv.at[u + 4], (ta, z_down, gy))

    def z_formed(u):
        img, r, s = split(u)
        return remote(PZ.at[img * 12 + 4 + s, r], PZ.at[img * 12 + s - 4, r], z_send.at[u],
                      z_recv.at[u - 4], (ta, z_up, gy))

    def z_any(u):
        return remote(V.at[0, pl.ds(0, rows)], V.at[0, pl.ds(0, rows)], z_send.at[u],
                      z_recv.at[u], (ta, z_up, gy))

    def y_vector(u):
        img, r, s = split(u)
        k = 2 * (s // 4) + lax.rem(s, 2)
        return remote(V.at[img * 16 + s, r], V.at[img * 16 + 12 + k, r], y_send.at[u],
                      y_recv.at[u + 2], (ta, gz, y_down))

    def y_formed(u):
        img, r, s = split(u)
        k = 2 * (s // 4) + lax.rem(s, 2)
        return remote(PY.at[img * 12 + s, r], PY.at[img * 12 + 8 + k, r], y_send.at[u],
                      y_recv.at[u - 2], (ta, gz, y_up))

    def y_any(u):
        return remote(V.at[0, pl.ds(0, rows)], V.at[0, pl.ds(0, rows)], y_send.at[u],
                      y_recv.at[u], (ta, gz, y_up))

    def send_time(u, source):
        near(u, source).start()

        @pl.when(u < 8)
        def _():
            block0(lax.rem(u, 8)).start()

    def send_z(target):
        @pl.when(lax.rem(target, 8) < 4)
        def _():
            z_formed(target + 4).start()

        @pl.when(lax.rem(target, 8) >= 4)
        def _():
            z_vector(target - 4).start()

    def send_y(u):
        y = lax.rem(u // 2, 2)

        @pl.when(y == 0)
        def _():
            y_vector(u).start()

        @pl.when(y == 1)
        def _():
            y_formed(u).start()

    def form(img, r, s, vector):
        block = jnp.concatenate([B[s], B[8 + s], B[16 + s]], axis=0)
        formed = times(vector, block).astype(jnp.bfloat16)
        width = vector.shape[1]
        PZ[img * 12 + 4 + s, r] = formed[:, :width]
        PY[img * 12 + s, r] = formed[:, width : 2 * width]
        PX[img * 8 + s, r] = formed[:, 2 * width :]

    @pl.loop(0, AHEAD)
    def _(u):
        send_time(u, src.at[lax.rem(u, 8)])

    fetch[0].wait()
    fetch[1].wait()

    @pl.loop(0, 8)
    def _(index):
        s = lax.rem(index + 4, 8)
        everything = pl.ds(0, PARTS * rows)
        form(0, everything, s, V[s])

        @pl.when(index < 4)
        def _():
            send_z(index)

        send_y(s)

    @pl.loop(4, Z_AHEAD)
    def _(u):
        send_z(u)

    @pl.loop(8, IMAGE)
    def _(u):
        send_y(u)

    for copy in fetch[2:]:
        copy.wait()
    total_r[...] = jnp.zeros_like(total_r)

    place = gz * n_gy + gy

    def gather(part):
        r = pl.ds(pl.multiple_of(part * rows, rows), rows)
        copies = [pltpu.make_async_copy(own_r.at[r], gathered.at[place, r], g_local.at[part])]
        for index, (a, b) in enumerate(others):
            oz, oy = other(a, b)
            copies.append(remote(own_r.at[r], gathered.at[place, r], g_send.at[part, index],
                                 g_recv.at[part, index], (ta, oz, oy)))
        return copies

    def result(u):
        img, r, s = split(u)
        return pltpu.make_async_copy(O.at[s, r], image.at[s, r], out_sem.at[u - IMAGE])

    def time_term(img, slot, s, r):
        term = times(T[img, slot, s, r], TB[slot, s])
        return jnp.where(slot == 1, term.astype(jnp.bfloat16).astype(jnp.float32), term)

    def begin(u):
        img, r, s = split(u)
        z, y, x = s // 4, lax.rem(s // 2, 2), lax.rem(s, 2)
        k = 2 * z + x
        base = img * 16
        y_next = base + (1 - y) * (s + 2) + y * (12 + k)
        y_from = img * 12 + y * (s - 2) + (1 - y) * (8 + k)
        flip = s + 1 - 2 * x

        @pl.when(u < 8)
        def _():
            block0(s).wait_recv()

        z_any(u).wait_recv()
        y_any(u).wait_recv()
        vectors = [V[base + s, r], V[base + flip, r], V[base + s + 4, r], V[y_next, r]]
        blocks = [C[s], F[16 + s], F[s], F[8 + s]]
        total = times(jnp.concatenate(vectors, axis=1), jnp.concatenate(blocks, axis=1))
        total = total + time_term(img, odd, s, r)
        for formed in (PX[img * 8 + flip, r], PZ[img * 12 + s, r], PY[y_from, r]):
            total = total + formed.astype(jnp.float32)
        early[lax.rem(u, 8)] = total

    def finish(u):
        img, r, s = split(u)
        far(u).wait_recv()
        total = early[lax.rem(u, 8)] + time_term(img, 1 - odd, s, r)
        value = total.astype(jnp.bfloat16)

        @pl.when(u < IMAGE)
        def _():
            V[16 + s, r] = value
            form(1, r, s, value)
            send_y(u + IMAGE)

        @pl.when(u >= IMAGE)
        def _():
            O[s, r] = value
            result(u).start()
            total_r[r] += times(value, R[s])

            @pl.when(s == 7)
            def _():
                own_r[r] = total_r[r].astype(jnp.bfloat16)
                for copy in gather(lax.rem(u // 8, PARTS)):
                    copy.start()

        @pl.when(u + Z_AHEAD < UNITS)
        def _():
            send_z(u + Z_AHEAD)

    @pl.loop(0, UNITS + LAG)
    def _(u):
        @pl.when(u < UNITS)
        def _():
            near(u, V.at[0]).wait_recv()
            far(u).start()

        @pl.when(u + AHEAD < UNITS)
        def _():
            v = u + AHEAD
            send_time(v, V.at[v // IMAGE * 16 + lax.rem(v, 8)])

        @pl.when(u < UNITS)
        def _():
            begin(u)

        @pl.when(u >= LAG)
        def _():
            finish(u - LAG)

    @pl.loop(0, UNITS)
    def _(u):
        near(u, V.at[0]).wait_send()
        far(u).wait_send()
        z_any(u).wait_send()
        y_any(u).wait_send()

    @pl.loop(0, 8)
    def _(s):
        block0(s).wait_send()

    @pl.loop(IMAGE, UNITS)
    def _(u):
        result(u).wait()

    @pl.loop(0, PARTS)
    def _(part):
        for copy in gather(part):
            copy.wait()


def write(image, gathered, image_out, gathered_out, held, inward, outward):
    parts = [(image.at[s], image_out.at[s]) for s in range(image.shape[0])]
    parts += [(gathered.at[s], gathered_out.at[s]) for s in range(gathered.shape[0])]
    reads = [pltpu.make_async_copy(a, held.at[i], inward.at[i]) for i, (a, _) in enumerate(parts)]
    writes = [pltpu.make_async_copy(held.at[i], b, outward.at[i]) for i, (_, b) in enumerate(parts)]
    for copy in reads:
        copy.start()
    for read, copy in zip(reads, writes):
        read.wait()
        copy.start()
    for copy in writes:
        copy.wait()


def written(image, gathered):
    count = image.shape[0] + gathered.shape[0]
    return pl.pallas_call(
        write,
        out_shape=(
            jax.ShapeDtypeStruct(image.shape, image.dtype),
            jax.ShapeDtypeStruct(gathered.shape, gathered.dtype),
        ),
        in_specs=[pl.BlockSpec(memory_space=pltpu.HBM)] * 2,
        out_specs=(pl.BlockSpec(memory_space=pltpu.HBM), pl.BlockSpec(memory_space=pltpu.HBM)),
        scratch_shapes=[
            pltpu.VMEM((count,) + image.shape[1:], image.dtype),
            pltpu.SemaphoreType.DMA((count,)),
            pltpu.SemaphoreType.DMA((count,)),
        ],
        compiler_params=pltpu.CompilerParams(vmem_limit_bytes=60 * 1024 * 1024),
    )(image, gathered)


def per_device(sizes, source_field, clover, forward, backward, restrict_blocks):
    n_ta, n_gz, n_gy = sizes
    rows, width = source_field.shape[-2:]
    field = (rows, width)
    block = (width, width)
    others = n_gz * n_gy - 1
    bf16 = jnp.bfloat16
    dma = pltpu.SemaphoreType.DMA
    image, gathered = pl.pallas_call(
        functools.partial(kernel, sizes),
        out_shape=(
            jax.ShapeDtypeStruct((8,) + field, bf16),
            jax.ShapeDtypeStruct((n_gz * n_gy,) + field, bf16),
        ),
        in_specs=[pl.BlockSpec(memory_space=pltpu.HBM)] * 5,
        out_specs=(pl.BlockSpec(memory_space=pltpu.HBM), pl.BlockSpec(memory_space=pltpu.HBM)),
        scratch_shapes=[
            pltpu.VMEM((32,) + field, bf16),
            pltpu.VMEM((2, 2, 8) + field, bf16),
            pltpu.VMEM((24,) + field, bf16),
            pltpu.VMEM((24,) + field, bf16),
            pltpu.VMEM((16,) + field, bf16),
            pltpu.VMEM((2, 8) + block, bf16),
            pltpu.VMEM((8,) + block, bf16),
            pltpu.VMEM((24,) + block, bf16),
            pltpu.VMEM((24,) + block, bf16),
            pltpu.VMEM((8,) + block, bf16),
            pltpu.VMEM((8,) + field, bf16),
            pltpu.VMEM((8, rows // PARTS, width), jnp.float32),
            pltpu.VMEM(field, jnp.float32),
            pltpu.VMEM(field, bf16),
            dma((UNITS,)), dma((UNITS,)), dma((UNITS,)), dma((UNITS,)),
            dma((8,)), dma((8,)),
            dma((UNITS,)), dma((UNITS,)), dma((UNITS,)), dma((UNITS,)),
            dma((6,)), dma((IMAGE,)), dma((PARTS, others)), dma((PARTS, others)), dma((PARTS,)),
        ],
        compiler_params=pltpu.CompilerParams(
            collective_id=0, has_side_effects=True, vmem_limit_bytes=60 * 1024 * 1024
        ),
    )(
        source_field.reshape((8,) + field),
        clover.reshape((8,) + block),
        forward.reshape((32,) + block),
        backward.reshape((32,) + block),
        restrict_blocks.reshape((8,) + block),
    )
    image, gathered = written(image, gathered)
    return image.reshape(source_field.shape), gathered.reshape((1, n_gz * n_gy) + field)


def solution(mesh):
    sizes = tuple(mesh.shape[axis] for axis in ("ta", "gz", "gy"))
    assert sizes[0] % 2 == 0 and sizes[0] >= 4
    return jax.shard_map(
        functools.partial(per_device, sizes),
        mesh=mesh,
        in_specs=(
            P("ta", "gz", "gy", None, None, None),
            P("ta", "gz", "gy", None, None, None),
            P(None, "ta", "gz", "gy", None, None, None),
            P(None, "ta", "gz", "gy", None, None, None),
            P("ta", "gz", "gy", None, None, None),
        ),
        out_specs=(P("ta", "gz", "gy", None, None, None), P("ta", None, None, None)),
        check_vma=False,
    )
```

```python
import functools

import jax
import jax.numpy as jnp
from jax import lax
from jax.experimental import pallas as pl
from jax.experimental.pallas import tpu as pltpu
from jax.sharding import PartitionSpec as P

MESH = pl.DeviceIdType.MESH
LAG = 2
AHEAD = 3
Z_AHEAD = 4
PARTS = 1
IMAGE = 8 * PARTS
UNITS = 2 * IMAGE


def times(vector, block):
    return lax.dot_general(
        vector, block, (((1,), (1,)), ((), ())), preferred_element_type=jnp.float32
    )


def kernel(
    sizes,
    src, clo, fwd, bwd, res,
    image, gathered,
    V, T, PZ, PY, PX, B0, C, F, B, R, O, total_r, own_r,
    near_send, near_recv, far_send, far_recv, b0_send, b0_recv,
    z_send, z_recv, y_send, y_recv, local, out_sem, g_send, g_recv, g_local,
):
    n_ta, n_gz, n_gy = sizes
    ta, gz, gy = lax.axis_index("ta"), lax.axis_index("gz"), lax.axis_index("gy")
    odd = lax.rem(ta, 2)
    partner = ta + 1 - 2 * odd
    beyond = lax.rem(ta + 2 - 4 * odd + n_ta, n_ta)
    following = lax.rem(ta + 1, n_ta)
    z_up, z_down = lax.rem(gz + 1, n_gz), lax.rem(gz + n_gz - 1, n_gz)
    y_up, y_down = lax.rem(gy + 1, n_gy), lax.rem(gy + n_gy - 1, n_gy)

    fetch = [
        pltpu.make_async_copy(src, V.at[pl.ds(0, 8)], local.at[0]),
        pltpu.make_async_copy(bwd.at[pl.ds(8, 24)], B, local.at[1]),
        pltpu.make_async_copy(fwd, F, local.at[2]),
        pltpu.make_async_copy(clo, C, local.at[3]),
        pltpu.make_async_copy(res, R, local.at[4]),
    ]
    for copy in fetch:
        copy.start()

    others = [(a, b) for a in range(n_gz) for b in range(n_gy) if (a, b) != (0, 0)]

    def other(a, b):
        return lax.rem(gz + a, n_gz), lax.rem(gz * 0 + gy + b, n_gy)

    barrier = pltpu.get_barrier_semaphore()
    for step in (1, 2, n_ta - 1, n_ta - 2):
        pl.semaphore_signal(
            barrier, inc=1, device_id=(lax.rem(ta + step, n_ta), gz, gy), device_id_type=MESH
        )
    for a, b in others:
        oz, oy = other(a, b)
        pl.semaphore_signal(barrier, inc=1, device_id=(ta, oz, oy), device_id_type=MESH)
    pl.semaphore_wait(barrier, 4 + len(others))

    def remote(source, target, send, recv, device):
        return pltpu.make_async_remote_copy(
            src_ref=source, dst_ref=target, send_sem=send, recv_sem=recv,
            device_id=device, device_id_type=MESH,
        )

    rows = src.shape[1] // PARTS

    def split(u):
        part = u // 8 % PARTS
        return u // IMAGE, pl.ds(part * rows, rows), u % 8

    def near(u, source):
        img, r, s = split(u)
        return remote(source.at[r], T.at[img, 1 - odd, s, r], near_send.at[u], near_recv.at[u],
                      (partner, gz, gy))

    def far(u):
        img, r, s = split(u)
        return remote(T.at[img, odd, s, r], T.at[img, 1 - odd, s, r], far_send.at[u],
                      far_recv.at[u], (beyond, gz, gy))

    def block0(s):
        return remote(bwd.at[s], B0.at[s], b0_send.at[s], b0_recv.at[s], (following, gz, gy))

    def z_vector(u):
        img, r, s = split(u)
        return remote(V.at[img * 16 + s, r], V.at[img * 16 + 8 + s, r], z_send.at[u],
                      z_recv.at[u + 4], (ta, z_down, gy))

    def z_formed(u):
        img, r, s = split(u)
        return remote(PZ.at[img * 12 + 4 + s, r], PZ.at[img * 12 + s - 4, r], z_send.at[u],
                      z_recv.at[u - 4], (ta, z_up, gy))

    def z_any(u):
        return remote(V.at[0, pl.ds(0, rows)], V.at[0, pl.ds(0, rows)], z_send.at[u],
                      z_recv.at[u], (ta, z_up, gy))

    def y_vector(u):
        img, r, s = split(u)
        k = 2 * (s // 4) + s % 2
        return remote(V.at[img * 16 + s, r], V.at[img * 16 + 12 + k, r], y_send.at[u],
                      y_recv.at[u + 2], (ta, gz, y_down))

    def y_formed(u):
        img, r, s = split(u)
        k = 2 * (s // 4) + s % 2
        return remote(PY.at[img * 12 + s, r], PY.at[img * 12 + 8 + k, r], y_send.at[u],
                      y_recv.at[u - 2], (ta, gz, y_up))

    def y_any(u):
        return remote(V.at[0, pl.ds(0, rows)], V.at[0, pl.ds(0, rows)], y_send.at[u],
                      y_recv.at[u], (ta, gz, y_up))

    def send_time(u, source):
        near(u, source).start()

        if u < 8:
            block0(u % 8).start()

    def send_z(target):
        if target % 8 < 4:
            z_formed(target + 4).start()

        if target % 8 >= 4:
            z_vector(target - 4).start()

    def send_y(u):
        y = (u // 2) % 2

        if y == 0:
            y_vector(u).start()

        if y == 1:
            y_formed(u).start()

    def form(img, r, s, vector):
        block = jnp.concatenate([B[s], B[8 + s], B[16 + s]], axis=0)
        formed = times(vector, block).astype(jnp.bfloat16)
        width = vector.shape[1]
        PZ[img * 12 + 4 + s, r] = formed[:, :width]
        PY[img * 12 + s, r] = formed[:, width : 2 * width]
        PX[img * 8 + s, r] = formed[:, 2 * width :]

    for u in range(0, AHEAD):
        send_time(u, src.at[u % 8])

    fetch[0].wait()
    fetch[1].wait()

    for index in range(0, 8):
        s = (index + 4) % 8
        everything = pl.ds(0, PARTS * rows)
        form(0, everything, s, V[s])

        if index < 4:
            send_z(index)

        send_y(s)

    for u in range(4, Z_AHEAD):
        send_z(u)

    for u in range(8, IMAGE):
        send_y(u)

    for copy in fetch[2:]:
        copy.wait()
    total_r[...] = jnp.zeros_like(total_r)

    place = gz * n_gy + gy

    def gather(part):
        r = pl.ds(part * rows, rows)
        copies = [pltpu.make_async_copy(own_r.at[r], gathered.at[place, r], g_local.at[part])]
        for index, (a, b) in enumerate(others):
            oz, oy = other(a, b)
            copies.append(remote(own_r.at[r], gathered.at[place, r], g_send.at[part, index],
                                 g_recv.at[part, index], (ta, oz, oy)))
        return copies

    def result(u):
        img, r, s = split(u)
        return pltpu.make_async_copy(O.at[s, r], image.at[s, r], out_sem.at[u - IMAGE])

    def finish(u):
        img, r, s = split(u)
        z, y, x = s // 4, (s // 2) % 2, s % 2
        k = 2 * z + x
        base = img * 16
        y_next = base + (1 - y) * (s + 2) + y * (12 + k)
        y_from = img * 12 + y * (s - 2) + (1 - y) * (8 + k)
        flip = s + 1 - 2 * x

        if u < 8:
            block0(s).wait_recv()

        z_any(u).wait_recv()
        y_any(u).wait_recv()
        far(u).wait_recv()
        vectors = [V[base + s, r], V[base + flip, r], V[base + s + 4, r], V[y_next, r],
                   T[img, 0, s, r]]
        blocks = [C[s], F[24 + s], F[8 + s], F[16 + s], F[s]]
        total = times(jnp.concatenate(vectors, axis=1), jnp.concatenate(blocks, axis=1))
        for formed in (PX[img * 8 + flip, r], PZ[img * 12 + s, r], PY[y_from, r],
                       times(T[img, 1, s, r], B0[s]).astype(jnp.bfloat16)):
            total = total + formed.astype(jnp.float32)
        value = total.astype(jnp.bfloat16)

        if u < IMAGE:
            V[16 + s, r] = value
            form(1, r, s, value)
            send_y(u + IMAGE)

        if u >= IMAGE:
            O[s, r] = value
            result(u).start()
            total_r[r] += times(value, R[s])

            if s == 7:
                own_r[r] = total_r[r].astype(jnp.bfloat16)
                for copy in gather(u // 8 % PARTS):
                    copy.start()

        if u + Z_AHEAD < UNITS:
            send_z(u + Z_AHEAD)

    for u in range(0, UNITS + LAG):
        if u < UNITS:
            near(u, V.at[0]).wait_recv()
            far(u).start()

        if u + AHEAD < UNITS:
            v = u + AHEAD
            send_time(v, V.at[v // IMAGE * 16 + v % 8])

        if u >= LAG:
            finish(u - LAG)

    for u in range(0, UNITS):
        near(u, V.at[0]).wait_send()
        far(u).wait_send()
        z_any(u).wait_send()
        y_any(u).wait_send()

    for s in range(0, 8):
        block0(s).wait_send()

    for u in range(IMAGE, UNITS):
        result(u).wait()

    for part in range(0, PARTS):
        for copy in gather(part):
            copy.wait()


def write(image, gathered, image_out, gathered_out, held, inward, outward):
    parts = [(image.at[s], image_out.at[s]) for s in range(image.shape[0])]
    parts += [(gathered.at[s], gathered_out.at[s]) for s in range(gathered.shape[0])]
    reads = [pltpu.make_async_copy(a, held.at[i], inward.at[i]) for i, (a, _) in enumerate(parts)]
    writes = [pltpu.make_async_copy(held.at[i], b, outward.at[i]) for i, (_, b) in enumerate(parts)]
    for copy in reads:
        copy.start()
    for read, copy in zip(reads, writes):
        read.wait()
        copy.start()
    for copy in writes:
        copy.wait()


def written(image, gathered):
    count = image.shape[0] + gathered.shape[0]
    return pl.pallas_call(
        write,
        out_shape=(
            jax.ShapeDtypeStruct(image.shape, image.dtype),
            jax.ShapeDtypeStruct(gathered.shape, gathered.dtype),
        ),
        in_specs=[pl.BlockSpec(memory_space=pltpu.HBM)] * 2,
        out_specs=(pl.BlockSpec(memory_space=pltpu.HBM), pl.BlockSpec(memory_space=pltpu.HBM)),
        scratch_shapes=[
            pltpu.VMEM((count,) + image.shape[1:], image.dtype),
            pltpu.SemaphoreType.DMA((count,)),
            pltpu.SemaphoreType.DMA((count,)),
        ],
        compiler_params=pltpu.CompilerParams(vmem_limit_bytes=60 * 1024 * 1024),
    )(image, gathered)


def per_device(sizes, source_field, clover, forward, backward, restrict_blocks):
    n_ta, n_gz, n_gy = sizes
    rows, width = source_field.shape[-2:]
    field = (rows, width)
    block = (width, width)
    others = n_gz * n_gy - 1
    bf16 = jnp.bfloat16
    dma = pltpu.SemaphoreType.DMA
    image, gathered = pl.pallas_call(
        functools.partial(kernel, sizes),
        out_shape=(
            jax.ShapeDtypeStruct((8,) + field, bf16),
            jax.ShapeDtypeStruct((n_gz * n_gy,) + field, bf16),
        ),
        in_specs=[pl.BlockSpec(memory_space=pltpu.HBM)] * 5,
        out_specs=(pl.BlockSpec(memory_space=pltpu.HBM), pl.BlockSpec(memory_space=pltpu.HBM)),
        scratch_shapes=[
            pltpu.VMEM((32,) + field, bf16),
            pltpu.VMEM((2, 2, 8) + field, bf16),
            pltpu.VMEM((24,) + field, bf16),
            pltpu.VMEM((24,) + field, bf16),
            pltpu.VMEM((16,) + field, bf16),
            pltpu.VMEM((8,) + block, bf16),
            pltpu.VMEM((8,) + block, bf16),
            pltpu.VMEM((32,) + block, bf16),
            pltpu.VMEM((24,) + block, bf16),
            pltpu.VMEM((8,) + block, bf16),
            pltpu.VMEM((8,) + field, bf16),
            pltpu.VMEM(field, jnp.float32),
            pltpu.VMEM(field, bf16),
            dma((UNITS,)), dma((UNITS,)), dma((UNITS,)), dma((UNITS,)),
            dma((8,)), dma((8,)),
            dma((UNITS,)), dma((UNITS,)), dma((UNITS,)), dma((UNITS,)),
            dma((5,)), dma((IMAGE,)), dma((PARTS, others)), dma((PARTS, others)), dma((PARTS,)),
        ],
        compiler_params=pltpu.CompilerParams(
            collective_id=0, has_side_effects=True, vmem_limit_bytes=60 * 1024 * 1024
        ),
    )(
        source_field.reshape((8,) + field),
        clover.reshape((8,) + block),
        forward.reshape((32,) + block),
        backward.reshape((32,) + block),
        restrict_blocks.reshape((8,) + block),
    )
    image, gathered = written(image, gathered)
    return image.reshape(source_field.shape), gathered.reshape((1, n_gz * n_gy) + field)


def solution(mesh):
    sizes = tuple(mesh.shape[axis] for axis in ("ta", "gz", "gy"))
    assert sizes[0] % 2 == 0 and sizes[0] >= 4
    return jax.shard_map(
        functools.partial(per_device, sizes),
        mesh=mesh,
        in_specs=(
            P("ta", "gz", "gy", None, None, None),
            P("ta", "gz", "gy", None, None, None),
            P(None, "ta", "gz", "gy", None, None, None),
            P(None, "ta", "gz", "gy", None, None, None),
            P("ta", "gz", "gy", None, None, None),
        ),
        out_specs=(P("ta", "gz", "gy", None, None, None), P("ta", None, None, None)),
        check_vma=False,
    )
```

```python
import functools

import jax
import jax.numpy as jnp
from jax import lax
from jax.experimental import pallas as pl
from jax.experimental.pallas import tpu as pltpu
from jax.sharding import PartitionSpec as P

MESH = pl.DeviceIdType.MESH
LAG = 4
AHEAD = 6
Z_AHEAD = 8
PARTS = 2
IMAGE = 8 * PARTS
UNITS = 2 * IMAGE


def times(vector, block):
    return lax.dot_general(
        vector, block, (((1,), (1,)), ((), ())), preferred_element_type=jnp.float32
    )


def kernel(
    sizes,
    src, clo, fwd, bwd, res,
    image, gathered,
    V, T, PZ, PY, PX, B0, C, F, B, R, O, total_r, own_r,
    near_send, near_recv, far_send, far_recv, b0_send, b0_recv,
    z_send, z_recv, y_send, y_recv, local, out_sem, g_send, g_recv, g_local,
):
    n_ta, n_gz, n_gy = sizes
    ta, gz, gy = lax.axis_index("ta"), lax.axis_index("gz"), lax.axis_index("gy")
    odd = lax.rem(ta, 2)
    partner = ta + 1 - 2 * odd
    beyond = lax.rem(ta + 2 - 4 * odd + n_ta, n_ta)
    z_up, z_down = lax.rem(gz + 1, n_gz), lax.rem(gz + n_gz - 1, n_gz)
    y_up, y_down = lax.rem(gy + 1, n_gy), lax.rem(gy + n_gy - 1, n_gy)

    fetch = [
        pltpu.make_async_copy(src, V.at[pl.ds(0, 8)], local.at[0]),
        pltpu.make_async_copy(bwd.at[pl.ds(8, 24)], B, local.at[1]),
        pltpu.make_async_copy(fwd, F, local.at[2]),
        pltpu.make_async_copy(clo, C, local.at[3]),
        pltpu.make_async_copy(res, R, local.at[4]),
    ]
    for copy in fetch:
        copy.start()

    others = [(a, b) for a in range(n_gz) for b in range(n_gy) if (a, b) != (0, 0)]

    def other(a, b):
        return lax.rem(gz + a, n_gz), lax.rem(gz * 0 + gy + b, n_gy)

    barrier = pltpu.get_barrier_semaphore()
    for neighbour in (partner, lax.rem(ta + 2, n_ta), lax.rem(ta + n_ta - 2, n_ta)):
        pl.semaphore_signal(barrier, inc=1, device_id=(neighbour, gz, gy), device_id_type=MESH)
    for a, b in others:
        oz, oy = other(a, b)
        pl.semaphore_signal(barrier, inc=1, device_id=(ta, oz, oy), device_id_type=MESH)
    pl.semaphore_wait(barrier, 3 + len(others))

    def remote(source, target, send, recv, device):
        return pltpu.make_async_remote_copy(
            src_ref=source, dst_ref=target, send_sem=send, recv_sem=recv,
            device_id=device, device_id_type=MESH,
        )

    rows = src.shape[1] // PARTS

    def split(u):
        part = lax.rem(u // 8, PARTS)
        return u // IMAGE, pl.ds(pl.multiple_of(part * rows, rows), rows), lax.rem(u, 8)

    def near(u, source):
        img, r, s = split(u)
        return remote(source.at[r], T.at[img, 0, s, r], near_send.at[u], near_recv.at[u],
                      (partner, gz, gy))

    def far(u):
        img, r, s = split(u)
        return remote(T.at[img, 2 - 2 * odd, s, r], T.at[img, 1, s, r], far_send.at[u],
                      far_recv.at[u], (beyond, gz, gy))

    def block0(s):
        return remote(bwd.at[s], B0.at[s], b0_send.at[s], b0_recv.at[s], (partner, gz, gy))

    def z_vector(u):
        img, r, s = split(u)
        return remote(V.at[img * 16 + s, r], V.at[img * 16 + 8 + s, r], z_send.at[u],
                      z_recv.at[u + 4], (ta, z_down, gy))

    def z_formed(u):
        img, r, s = split(u)
        return remote(PZ.at[img * 12 + 4 + s, r], PZ.at[img * 12 + s - 4, r], z_send.at[u],
                      z_recv.at[u - 4], (ta, z_up, gy))

    def z_any(u):
        return remote(V.at[0, pl.ds(0, rows)], V.at[0, pl.ds(0, rows)], z_send.at[u],
                      z_recv.at[u], (ta, z_up, gy))

    def y_vector(u):
        img, r, s = split(u)
        k = 2 * (s // 4) + lax.rem(s, 2)
        return remote(V.at[img * 16 + s, r], V.at[img * 16 + 12 + k, r], y_send.at[u],
                      y_recv.at[u + 2], (ta, gz, y_down))

    def y_formed(u):
        img, r, s = split(u)
        k = 2 * (s // 4) + lax.rem(s, 2)
        return remote(PY.at[img * 12 + s, r], PY.at[img * 12 + 8 + k, r], y_send.at[u],
                      y_recv.at[u - 2], (ta, gz, y_up))

    def y_any(u):
        return remote(V.at[0, pl.ds(0, rows)], V.at[0, pl.ds(0, rows)], y_send.at[u],
                      y_recv.at[u], (ta, gz, y_up))

    def send_time(u, source):
        @pl.when(u < 8)
        def _():
            block0(lax.rem(u, 8)).start()

        near(u, source).start()

    def send_z(target):
        @pl.when(lax.rem(target, 8) < 4)
        def _():
            z_formed(target + 4).start()

        @pl.when(lax.rem(target, 8) >= 4)
        def _():
            z_vector(target - 4).start()

    def send_y(u):
        y = lax.rem(u // 2, 2)

        @pl.when(y == 0)
        def _():
            y_vector(u).start()

        @pl.when(y == 1)
        def _():
            y_formed(u).start()

    def form(img, r, s, vector):
        block = jnp.concatenate([B[s], B[8 + s], B[16 + s]], axis=0)
        formed = times(vector, block).astype(jnp.bfloat16)
        width = vector.shape[1]
        PZ[img * 12 + 4 + s, r] = formed[:, :width]
        PY[img * 12 + s, r] = formed[:, width : 2 * width]
        PX[img * 8 + s, r] = formed[:, 2 * width :]

    @pl.loop(0, AHEAD)
    def _(u):
        send_time(u, src.at[lax.rem(u, 8)])

    fetch[0].wait()
    fetch[1].wait()

    @pl.loop(0, 8)
    def _(index):
        s = lax.rem(index + 4, 8)
        everything = pl.ds(0, PARTS * rows)
        form(0, everything, s, V[s])

        @pl.when(index < 4)
        def _():
            send_z(index)

        send_y(s)

    @pl.loop(4, Z_AHEAD)
    def _(u):
        send_z(u)

    @pl.loop(8, IMAGE)
    def _(u):
        send_y(u)

    for copy in fetch[2:]:
        copy.wait()
    total_r[...] = jnp.zeros_like(total_r)

    place = gz * n_gy + gy

    def gather(part):
        r = pl.ds(pl.multiple_of(part * rows, rows), rows)
        copies = [pltpu.make_async_copy(own_r.at[r], gathered.at[place, r], g_local.at[part])]
        for index, (a, b) in enumerate(others):
            oz, oy = other(a, b)
            copies.append(remote(own_r.at[r], gathered.at[place, r], g_send.at[part, index],
                                 g_recv.at[part, index], (ta, oz, oy)))
        return copies

    def result(u):
        img, r, s = split(u)
        return pltpu.make_async_copy(O.at[s, r], image.at[s, r], out_sem.at[u - IMAGE])

    def finish(u):
        img, r, s = split(u)
        z, y, x = s // 4, lax.rem(s // 2, 2), lax.rem(s, 2)
        k = 2 * z + x
        base = img * 16
        y_next = base + (1 - y) * (s + 2) + y * (12 + k)
        y_from = img * 12 + y * (s - 2) + (1 - y) * (8 + k)
        flip = s + 1 - 2 * x

        z_any(u).wait_recv()
        y_any(u).wait_recv()
        far(u).wait_recv()
        vectors = [V[base + s, r], V[base + flip, r], V[base + s + 4, r], V[y_next, r],
                   T[img, odd, s, r]]
        blocks = [C[s], F[24 + s], F[8 + s], F[16 + s], F[s]]
        total = times(jnp.concatenate(vectors, axis=1), jnp.concatenate(blocks, axis=1))
        for formed in (PX[img * 8 + flip, r], PZ[img * 12 + s, r], PY[y_from, r],
                       T[img, 1 + odd, s, r]):
            total = total + formed.astype(jnp.float32)
        value = total.astype(jnp.bfloat16)

        @pl.when(u < IMAGE)
        def _():
            V[16 + s, r] = value
            form(1, r, s, value)
            send_y(u + IMAGE)

        @pl.when(u >= IMAGE)
        def _():
            O[s, r] = value
            result(u).start()
            total_r[r] += times(value, R[s])

            @pl.when(s == 7)
            def _():
                own_r[r] = total_r[r].astype(jnp.bfloat16)
                for copy in gather(lax.rem(u // 8, PARTS)):
                    copy.start()

        @pl.when(u + Z_AHEAD < UNITS)
        def _():
            send_z(u + Z_AHEAD)

    @pl.loop(0, UNITS + LAG)
    def _(u):
        @pl.when(u < UNITS)
        def _():
            img, r, s = split(u)
            near(u, V.at[0]).wait_recv()

            @pl.when(u < 8)
            def _():
                block0(s).wait_recv()

            T[img, 2, s, r] = times(T[img, 0, s, r], B0[s]).astype(jnp.bfloat16)
            far(u).start()

        @pl.when(u + AHEAD < UNITS)
        def _():
            v = u + AHEAD
            send_time(v, V.at[v // IMAGE * 16 + lax.rem(v, 8)])

        @pl.when(u >= LAG)
        def _():
            finish(u - LAG)

    @pl.loop(0, UNITS)
    def _(u):
        near(u, V.at[0]).wait_send()
        far(u).wait_send()
        z_any(u).wait_send()
        y_any(u).wait_send()

    @pl.loop(0, 8)
    def _(s):
        block0(s).wait_send()

    @pl.loop(IMAGE, UNITS)
    def _(u):
        result(u).wait()

    @pl.loop(0, PARTS)
    def _(part):
        for copy in gather(part):
            copy.wait()


def write(image, gathered, image_out, gathered_out, held, inward, outward):
    parts = [(image.at[s], image_out.at[s]) for s in range(image.shape[0])]
    parts += [(gathered.at[s], gathered_out.at[s]) for s in range(gathered.shape[0])]
    reads = [pltpu.make_async_copy(a, held.at[i], inward.at[i]) for i, (a, _) in enumerate(parts)]
    writes = [pltpu.make_async_copy(held.at[i], b, outward.at[i]) for i, (_, b) in enumerate(parts)]
    for copy in reads:
        copy.start()
    for read, copy in zip(reads, writes):
        read.wait()
        copy.start()
    for copy in writes:
        copy.wait()


def written(image, gathered):
    count = image.shape[0] + gathered.shape[0]
    return pl.pallas_call(
        write,
        out_shape=(
            jax.ShapeDtypeStruct(image.shape, image.dtype),
            jax.ShapeDtypeStruct(gathered.shape, gathered.dtype),
        ),
        in_specs=[pl.BlockSpec(memory_space=pltpu.HBM)] * 2,
        out_specs=(pl.BlockSpec(memory_space=pltpu.HBM), pl.BlockSpec(memory_space=pltpu.HBM)),
        scratch_shapes=[
            pltpu.VMEM((count,) + image.shape[1:], image.dtype),
            pltpu.SemaphoreType.DMA((count,)),
            pltpu.SemaphoreType.DMA((count,)),
        ],
        compiler_params=pltpu.CompilerParams(vmem_limit_bytes=60 * 1024 * 1024),
    )(image, gathered)


def per_device(sizes, source_field, clover, forward, backward, restrict_blocks):
    n_ta, n_gz, n_gy = sizes
    rows, width = source_field.shape[-2:]
    field = (rows, width)
    block = (width, width)
    others = n_gz * n_gy - 1
    bf16 = jnp.bfloat16
    dma = pltpu.SemaphoreType.DMA
    image, gathered = pl.pallas_call(
        functools.partial(kernel, sizes),
        out_shape=(
            jax.ShapeDtypeStruct((8,) + field, bf16),
            jax.ShapeDtypeStruct((n_gz * n_gy,) + field, bf16),
        ),
        in_specs=[pl.BlockSpec(memory_space=pltpu.HBM)] * 5,
        out_specs=(pl.BlockSpec(memory_space=pltpu.HBM), pl.BlockSpec(memory_space=pltpu.HBM)),
        scratch_shapes=[
            pltpu.VMEM((32,) + field, bf16),
            pltpu.VMEM((2, 3, 8) + field, bf16),
            pltpu.VMEM((24,) + field, bf16),
            pltpu.VMEM((24,) + field, bf16),
            pltpu.VMEM((16,) + field, bf16),
            pltpu.VMEM((8,) + block, bf16),
            pltpu.VMEM((8,) + block, bf16),
            pltpu.VMEM((32,) + block, bf16),
            pltpu.VMEM((24,) + block, bf16),
            pltpu.VMEM((8,) + block, bf16),
            pltpu.VMEM((8,) + field, bf16),
            pltpu.VMEM(field, jnp.float32),
            pltpu.VMEM(field, bf16),
            dma((UNITS,)), dma((UNITS,)), dma((UNITS,)), dma((UNITS,)),
            dma((8,)), dma((8,)),
            dma((UNITS,)), dma((UNITS,)), dma((UNITS,)), dma((UNITS,)),
            dma((5,)), dma((IMAGE,)), dma((PARTS, others)), dma((PARTS, others)), dma((PARTS,)),
        ],
        compiler_params=pltpu.CompilerParams(
            collective_id=0, has_side_effects=True, vmem_limit_bytes=60 * 1024 * 1024
        ),
    )(
        source_field.reshape((8,) + field),
        clover.reshape((8,) + block),
        forward.reshape((32,) + block),
        backward.reshape((32,) + block),
        restrict_blocks.reshape((8,) + block),
    )
    image, gathered = written(image, gathered)
    return image.reshape(source_field.shape), gathered.reshape((1, n_gz * n_gy) + field)


def solution(mesh):
    sizes = tuple(mesh.shape[axis] for axis in ("ta", "gz", "gy"))
    assert sizes[0] % 2 == 0 and sizes[0] >= 4
    return jax.shard_map(
        functools.partial(per_device, sizes),
        mesh=mesh,
        in_specs=(
            P("ta", "gz", "gy", None, None, None),
            P("ta", "gz", "gy", None, None, None),
            P(None, "ta", "gz", "gy", None, None, None),
            P(None, "ta", "gz", "gy", None, None, None),
            P("ta", "gz", "gy", None, None, None),
        ),
        out_specs=(P("ta", "gz", "gy", None, None, None), P("ta", None, None, None)),
        check_vma=False,
    )
```

```python
import functools

import jax
import jax.numpy as jnp
from jax import lax
from jax.experimental import pallas as pl
from jax.experimental.pallas import tpu as pltpu
from jax.sharding import PartitionSpec as P

MESH = pl.DeviceIdType.MESH
LAG = 2
AHEAD = 3
Z_AHEAD = 4
UNITS = 16
PIECES = 17


def times(vector, block):
    return lax.dot_general(
        vector, block, (((1,), (1,)), ((), ())), preferred_element_type=jnp.float32
    )


def kernel(
    sizes,
    src, clo, fwd, bwd, res,
    image, gathered,
    V, T, PZ, PY, PX, B0, C, F, B, R, O, total_r, own_r,
    near_send, near_recv, far_send, far_recv, b0_send, b0_recv,
    z_send, z_recv, y_send, y_recv, local, out_sem, g_send, g_recv, g_local,
):
    n_ta, n_gz, n_gy = sizes
    ta, gz, gy = lax.axis_index("ta"), lax.axis_index("gz"), lax.axis_index("gy")
    odd = lax.rem(ta, 2)
    partner = ta + 1 - 2 * odd
    beyond = lax.rem(ta + 2 - 4 * odd + n_ta, n_ta)
    z_up, z_down = lax.rem(gz + 1, n_gz), lax.rem(gz + n_gz - 1, n_gz)
    y_up, y_down = lax.rem(gy + 1, n_gy), lax.rem(gy + n_gy - 1, n_gy)

    fetch = [
        pltpu.make_async_copy(src, V.at[pl.ds(0, 8)], local.at[0]),
        pltpu.make_async_copy(bwd.at[pl.ds(8, 24)], B, local.at[1]),
        pltpu.make_async_copy(fwd, F, local.at[2]),
        pltpu.make_async_copy(clo, C, local.at[3]),
        pltpu.make_async_copy(res, R, local.at[4]),
    ]
    for copy in fetch:
        copy.start()

    others = [(a, b) for a in range(n_gz) for b in range(n_gy) if (a, b) != (0, 0)]

    def other(a, b):
        return lax.rem(gz + a, n_gz), lax.rem(gz * 0 + gy + b, n_gy)

    barrier = pltpu.get_barrier_semaphore()
    for neighbour in (partner, lax.rem(ta + 2, n_ta), lax.rem(ta + n_ta - 2, n_ta)):
        pl.semaphore_signal(barrier, inc=1, device_id=(neighbour, gz, gy), device_id_type=MESH)
    for a, b in others:
        oz, oy = other(a, b)
        pl.semaphore_signal(barrier, inc=1, device_id=(ta, oz, oy), device_id_type=MESH)
    pl.semaphore_wait(barrier, 3 + len(others))

    def remote(source, target, send, recv, device):
        return pltpu.make_async_remote_copy(
            src_ref=source, dst_ref=target, send_sem=send, recv_sem=recv,
            device_id=device, device_id_type=MESH,
        )

    rows = src.shape[1]
    half = rows // 2

    def split(u):
        return u // 8, pl.ds(0, rows), u % 8

    def piece(q):
        if q < UNITS - 1:
            return q // 8, pl.ds(0, rows), q % 8
        return 1, pl.ds((q - UNITS + 1) * half, half), 7

    def near(q, source):
        img, r, s = piece(q)
        return remote(source.at[r], T.at[img, 0, s, r], near_send.at[q], near_recv.at[q],
                      (partner, gz, gy))

    def far(q):
        img, r, s = piece(q)
        return remote(T.at[img, 2 - 2 * odd, s, r], T.at[img, 1, s, r], far_send.at[q],
                      far_recv.at[q], (beyond, gz, gy))

    def block0(s):
        return remote(bwd.at[s], B0.at[s], b0_send.at[s], b0_recv.at[s], (partner, gz, gy))

    def z_vector(u):
        img, r, s = split(u)
        return remote(V.at[img * 16 + s, r], V.at[img * 16 + 8 + s, r], z_send.at[u],
                      z_recv.at[u + 4], (ta, z_down, gy))

    def z_formed(u):
        img, r, s = split(u)
        return remote(PZ.at[img * 12 + 4 + s, r], PZ.at[img * 12 + s - 4, r], z_send.at[u],
                      z_recv.at[u - 4], (ta, z_up, gy))

    def z_any(u):
        return remote(V.at[0, pl.ds(0, rows)], V.at[0, pl.ds(0, rows)], z_send.at[u],
                      z_recv.at[u], (ta, z_up, gy))

    def y_vector(u):
        img, r, s = split(u)
        k = 2 * (s // 4) + s % 2
        return remote(V.at[img * 16 + s, r], V.at[img * 16 + 12 + k, r], y_send.at[u],
                      y_recv.at[u + 2], (ta, gz, y_down))

    def y_formed(u):
        img, r, s = split(u)
        k = 2 * (s // 4) + s % 2
        return remote(PY.at[img * 12 + s, r], PY.at[img * 12 + 8 + k, r], y_send.at[u],
                      y_recv.at[u - 2], (ta, gz, y_up))

    def y_any(u):
        return remote(V.at[0, pl.ds(0, rows)], V.at[0, pl.ds(0, rows)], y_send.at[u],
                      y_recv.at[u], (ta, gz, y_up))

    def send_time(u, source):
        if u < 8:
            block0(u % 8).start()

        near(u, source).start()

    def send_z(target):
        if target % 8 < 4:
            z_formed(target + 4).start()

        if target % 8 >= 4:
            z_vector(target - 4).start()

    def send_y(u):
        y = (u // 2) % 2

        if y == 0:
            y_vector(u).start()

        if y == 1:
            y_formed(u).start()

    def form(img, r, s, vector):
        block = jnp.concatenate([B[s], B[8 + s], B[16 + s]], axis=0)
        formed = times(vector, block).astype(jnp.bfloat16)
        width = vector.shape[1]
        PZ[img * 12 + 4 + s, r] = formed[:, :width]
        PY[img * 12 + s, r] = formed[:, width : 2 * width]
        PX[img * 8 + s, r] = formed[:, 2 * width :]

    for u in range(0, AHEAD):
        send_time(u, src.at[u % 8])

    fetch[0].wait()
    fetch[1].wait()

    for index in range(0, 8):
        s = (index + 4) % 8
        everything = pl.ds(0, rows)
        form(0, everything, s, V[s])

        if index < 4:
            send_z(index)

        send_y(s)

    for copy in fetch[2:]:
        copy.wait()
    total_r[...] = jnp.zeros_like(total_r)

    place = gz * n_gy + gy

    def gather(part):
        r = pl.ds(part * half, half)
        copies = [pltpu.make_async_copy(own_r.at[r], gathered.at[place, r], g_local.at[part])]
        for index, (a, b) in enumerate(others):
            oz, oy = other(a, b)
            copies.append(remote(own_r.at[r], gathered.at[place, r], g_send.at[part, index],
                                 g_recv.at[part, index], (ta, oz, oy)))
        return copies

    def result(q):
        img, r, s = piece(q)
        return pltpu.make_async_copy(O.at[s, r], image.at[s, r], out_sem.at[q - 8])

    def finish(q):
        img, r, s = piece(q)
        u = img * 8 + s
        z, y, x = s // 4, (s // 2) % 2, s % 2
        k = 2 * z + x
        base = img * 16
        y_next = base + (1 - y) * (s + 2) + y * (12 + k)
        y_from = img * 12 + y * (s - 2) + (1 - y) * (8 + k)
        flip = s + 1 - 2 * x

        if q == u:
            z_any(u).wait_recv()
            y_any(u).wait_recv()
        far(q).wait_recv()
        vectors = [V[base + s, r], V[base + flip, r], V[base + s + 4, r], V[y_next, r],
                   T[img, odd, s, r]]
        blocks = [C[s], F[24 + s], F[8 + s], F[16 + s], F[s]]
        total = times(jnp.concatenate(vectors, axis=1), jnp.concatenate(blocks, axis=1))
        for formed in (PX[img * 8 + flip, r], PZ[img * 12 + s, r], PY[y_from, r],
                       T[img, 1 + odd, s, r]):
            total = total + formed.astype(jnp.float32)
        value = total.astype(jnp.bfloat16)

        if img == 0:
            V[16 + s, r] = value
            form(1, r, s, value)
            send_y(u + 8)
        else:
            O[s, r] = value
            result(q).start()
            total_r[r] += times(value, R[s])

            if s == 7:
                own_r[r] = total_r[r].astype(jnp.bfloat16)
                for copy in gather(q - UNITS + 1):
                    copy.start()

        if u + Z_AHEAD < UNITS:
            send_z(u + Z_AHEAD)

    for q in range(PIECES + LAG):
        if q < PIECES:
            img, r, s = piece(q)
            near(q, V.at[0]).wait_recv()

            if q < 8:
                block0(s).wait_recv()

            T[img, 2, s, r] = times(T[img, 0, s, r], B0[s]).astype(jnp.bfloat16)
            far(q).start()

        if q + AHEAD < PIECES:
            later, _, site = piece(q + AHEAD)
            send_time(q + AHEAD, V.at[later * 16 + site])

        if q >= LAG:
            finish(q - LAG)

    for u in range(UNITS):
        z_any(u).wait_send()
        y_any(u).wait_send()

    for q in range(PIECES):
        near(q, V.at[0]).wait_send()
        far(q).wait_send()

    for s in range(8):
        block0(s).wait_send()

    for q in range(8, PIECES):
        result(q).wait()

    for part in range(2):
        for copy in gather(part):
            copy.wait()


def write(image, gathered, image_out, gathered_out, held, inward, outward):
    parts = [(image.at[s], image_out.at[s]) for s in range(image.shape[0])]
    parts += [(gathered.at[s], gathered_out.at[s]) for s in range(gathered.shape[0])]
    reads = [pltpu.make_async_copy(a, held.at[i], inward.at[i]) for i, (a, _) in enumerate(parts)]
    writes = [pltpu.make_async_copy(held.at[i], b, outward.at[i]) for i, (_, b) in enumerate(parts)]
    for copy in reads:
        copy.start()
    for read, copy in zip(reads, writes):
        read.wait()
        copy.start()
    for copy in writes:
        copy.wait()


def written(image, gathered):
    count = image.shape[0] + gathered.shape[0]
    return pl.pallas_call(
        write,
        out_shape=(
            jax.ShapeDtypeStruct(image.shape, image.dtype),
            jax.ShapeDtypeStruct(gathered.shape, gathered.dtype),
        ),
        in_specs=[pl.BlockSpec(memory_space=pltpu.HBM)] * 2,
        out_specs=(pl.BlockSpec(memory_space=pltpu.HBM), pl.BlockSpec(memory_space=pltpu.HBM)),
        scratch_shapes=[
            pltpu.VMEM((count,) + image.shape[1:], image.dtype),
            pltpu.SemaphoreType.DMA((count,)),
            pltpu.SemaphoreType.DMA((count,)),
        ],
        compiler_params=pltpu.CompilerParams(vmem_limit_bytes=60 * 1024 * 1024),
    )(image, gathered)


def per_device(sizes, source_field, clover, forward, backward, restrict_blocks):
    n_ta, n_gz, n_gy = sizes
    rows, width = source_field.shape[-2:]
    field = (rows, width)
    block = (width, width)
    others = n_gz * n_gy - 1
    bf16 = jnp.bfloat16
    dma = pltpu.SemaphoreType.DMA
    image, gathered = pl.pallas_call(
        functools.partial(kernel, sizes),
        out_shape=(
            jax.ShapeDtypeStruct((8,) + field, bf16),
            jax.ShapeDtypeStruct((n_gz * n_gy,) + field, bf16),
        ),
        in_specs=[pl.BlockSpec(memory_space=pltpu.HBM)] * 5,
        out_specs=(pl.BlockSpec(memory_space=pltpu.HBM), pl.BlockSpec(memory_space=pltpu.HBM)),
        scratch_shapes=[
            pltpu.VMEM((32,) + field, bf16),
            pltpu.VMEM((2, 3, 8) + field, bf16),
            pltpu.VMEM((24,) + field, bf16),
            pltpu.VMEM((24,) + field, bf16),
            pltpu.VMEM((16,) + field, bf16),
            pltpu.VMEM((8,) + block, bf16),
            pltpu.VMEM((8,) + block, bf16),
            pltpu.VMEM((32,) + block, bf16),
            pltpu.VMEM((24,) + block, bf16),
            pltpu.VMEM((8,) + block, bf16),
            pltpu.VMEM((8,) + field, bf16),
            pltpu.VMEM(field, jnp.float32),
            pltpu.VMEM(field, bf16),
            dma((PIECES,)), dma((PIECES,)), dma((PIECES,)), dma((PIECES,)),
            dma((8,)), dma((8,)),
            dma((UNITS,)), dma((UNITS,)), dma((UNITS,)), dma((UNITS,)),
            dma((5,)), dma((PIECES - 8,)), dma((2, others)), dma((2, others)), dma((2,)),
        ],
        compiler_params=pltpu.CompilerParams(
            collective_id=0, has_side_effects=True, vmem_limit_bytes=60 * 1024 * 1024
        ),
    )(
        source_field.reshape((8,) + field),
        clover.reshape((8,) + block),
        forward.reshape((32,) + block),
        backward.reshape((32,) + block),
        restrict_blocks.reshape((8,) + block),
    )
    image, gathered = written(image, gathered)
    return image.reshape(source_field.shape), gathered.reshape((1, n_gz * n_gy) + field)


def solution(mesh):
    sizes = tuple(mesh.shape[axis] for axis in ("ta", "gz", "gy"))
    assert sizes[0] % 2 == 0 and sizes[0] >= 4
    return jax.shard_map(
        functools.partial(per_device, sizes),
        mesh=mesh,
        in_specs=(
            P("ta", "gz", "gy", None, None, None),
            P("ta", "gz", "gy", None, None, None),
            P(None, "ta", "gz", "gy", None, None, None),
            P(None, "ta", "gz", "gy", None, None, None),
            P("ta", "gz", "gy", None, None, None),
        ),
        out_specs=(P("ta", "gz", "gy", None, None, None), P("ta", None, None, None)),
        check_vma=False,
    )
```

```python
import functools

import jax
import jax.numpy as jnp
from jax import lax
from jax.experimental import pallas as pl
from jax.experimental.pallas import tpu as pltpu
from jax.sharding import PartitionSpec as P

MESH = pl.DeviceIdType.MESH
LAG = 4
AHEAD = 3
Z_AHEAD = 4
UNITS = 16
PIECES = 17


def times(vector, block):
    return lax.dot_general(
        vector, block, (((1,), (1,)), ((), ())), preferred_element_type=jnp.float32
    )


def kernel(
    sizes,
    src, clo, fwd, bwd, res,
    image, gathered,
    V, T, PZ, PY, PX, B0, C, F, B, R, O, total_r, own_r,
    near_send, near_recv, far_send, far_recv, b0_send, b0_recv,
    z_send, z_recv, y_send, y_recv, local, out_sem, g_send, g_recv, g_local,
):
    n_ta, n_gz, n_gy = sizes
    ta, gz, gy = lax.axis_index("ta"), lax.axis_index("gz"), lax.axis_index("gy")
    odd = lax.rem(ta, 2)
    partner = ta + 1 - 2 * odd
    beyond = lax.rem(ta + 2 - 4 * odd + n_ta, n_ta)
    z_up, z_down = lax.rem(gz + 1, n_gz), lax.rem(gz + n_gz - 1, n_gz)
    y_up, y_down = lax.rem(gy + 1, n_gy), lax.rem(gy + n_gy - 1, n_gy)

    fetch = [
        pltpu.make_async_copy(src, V.at[pl.ds(0, 8)], local.at[0]),
        pltpu.make_async_copy(bwd.at[pl.ds(8, 24)], B, local.at[1]),
        pltpu.make_async_copy(fwd, F, local.at[2]),
        pltpu.make_async_copy(clo, C, local.at[3]),
        pltpu.make_async_copy(res, R, local.at[4]),
    ]
    for copy in fetch:
        copy.start()

    others = [(a, b) for a in range(n_gz) for b in range(n_gy) if (a, b) != (0, 0)]

    def other(a, b):
        return lax.rem(gz + a, n_gz), lax.rem(gz * 0 + gy + b, n_gy)

    barrier = pltpu.get_barrier_semaphore()
    for neighbour in (partner, lax.rem(ta + 2, n_ta), lax.rem(ta + n_ta - 2, n_ta)):
        pl.semaphore_signal(barrier, inc=1, device_id=(neighbour, gz, gy), device_id_type=MESH)
    for a, b in others:
        oz, oy = other(a, b)
        pl.semaphore_signal(barrier, inc=1, device_id=(ta, oz, oy), device_id_type=MESH)
    pl.semaphore_wait(barrier, 3 + len(others))

    def remote(source, target, send, recv, device):
        return pltpu.make_async_remote_copy(
            src_ref=source, dst_ref=target, send_sem=send, recv_sem=recv,
            device_id=device, device_id_type=MESH,
        )

    rows = src.shape[1]
    half = rows // 2

    def split(u):
        return u // 8, pl.ds(0, rows), u % 8

    def piece(q):
        if q < UNITS - 1:
            return q // 8, pl.ds(0, rows), q % 8
        return 1, pl.ds((q - UNITS + 1) * half, half), 7

    def near(q, source):
        img, r, s = piece(q)
        return remote(source.at[r], T.at[img, 0, s, r], near_send.at[q], near_recv.at[q],
                      (partner, gz, gy))

    def far(q):
        img, r, s = piece(q)
        return remote(T.at[img, 2 - 2 * odd, s, r], T.at[img, 1, s, r], far_send.at[q],
                      far_recv.at[q], (beyond, gz, gy))

    def block0(s):
        return remote(bwd.at[s], B0.at[s], b0_send.at[s], b0_recv.at[s], (partner, gz, gy))

    def z_vector(u):
        img, r, s = split(u)
        return remote(V.at[img * 16 + s, r], V.at[img * 16 + 8 + s, r], z_send.at[u],
                      z_recv.at[u + 4], (ta, z_down, gy))

    def z_formed(u):
        img, r, s = split(u)
        return remote(PZ.at[img * 12 + 4 + s, r], PZ.at[img * 12 + s - 4, r], z_send.at[u],
                      z_recv.at[u - 4], (ta, z_up, gy))

    def z_any(u):
        return remote(V.at[0, pl.ds(0, rows)], V.at[0, pl.ds(0, rows)], z_send.at[u],
                      z_recv.at[u], (ta, z_up, gy))

    def y_vector(u):
        img, r, s = split(u)
        k = 2 * (s // 4) + s % 2
        return remote(V.at[img * 16 + s, r], V.at[img * 16 + 12 + k, r], y_send.at[u],
                      y_recv.at[u + 2], (ta, gz, y_down))

    def y_formed(u):
        img, r, s = split(u)
        k = 2 * (s // 4) + s % 2
        return remote(PY.at[img * 12 + s, r], PY.at[img * 12 + 8 + k, r], y_send.at[u],
                      y_recv.at[u - 2], (ta, gz, y_up))

    def y_any(u):
        return remote(V.at[0, pl.ds(0, rows)], V.at[0, pl.ds(0, rows)], y_send.at[u],
                      y_recv.at[u], (ta, gz, y_up))

    def send_time(u, source):
        if u < 8:
            block0(u % 8).start()

        near(u, source).start()

    def send_z(target):
        if target % 8 < 4:
            z_formed(target + 4).start()

        if target % 8 >= 4:
            z_vector(target - 4).start()

    def send_y(u):
        y = (u // 2) % 2

        if y == 0:
            y_vector(u).start()

        if y == 1:
            y_formed(u).start()

    def form(img, r, s, vector):
        block = jnp.concatenate([B[s], B[8 + s], B[16 + s]], axis=0)
        formed = times(vector, block).astype(jnp.bfloat16)
        width = vector.shape[1]
        PZ[img * 12 + 4 + s, r] = formed[:, :width]
        PY[img * 12 + s, r] = formed[:, width : 2 * width]
        PX[img * 8 + s, r] = formed[:, 2 * width :]

    for u in range(0, AHEAD):
        send_time(u, src.at[u % 8])

    fetch[0].wait()
    fetch[1].wait()

    for index in range(0, 8):
        s = (index + 4) % 8
        everything = pl.ds(0, rows)
        form(0, everything, s, V[s])

        if index < 4:
            send_z(index)

        send_y(s)

    for copy in fetch[2:]:
        copy.wait()
    total_r[...] = jnp.zeros_like(total_r)

    place = gz * n_gy + gy

    def gather(part):
        r = pl.ds(part * half, half)
        copies = [pltpu.make_async_copy(own_r.at[r], gathered.at[place, r], g_local.at[part])]
        for index, (a, b) in enumerate(others):
            oz, oy = other(a, b)
            copies.append(remote(own_r.at[r], gathered.at[place, r], g_send.at[part, index],
                                 g_recv.at[part, index], (ta, oz, oy)))
        return copies

    def result(q):
        img, r, s = piece(q)
        return pltpu.make_async_copy(O.at[s, r], image.at[s, r], out_sem.at[q - 8])

    def finish(q):
        img, r, s = piece(q)
        u = img * 8 + s
        z, y, x = s // 4, (s // 2) % 2, s % 2
        k = 2 * z + x
        base = img * 16
        y_next = base + (1 - y) * (s + 2) + y * (12 + k)
        y_from = img * 12 + y * (s - 2) + (1 - y) * (8 + k)
        flip = s + 1 - 2 * x

        if q == u:
            z_any(u).wait_recv()
            y_any(u).wait_recv()
        far(q).wait_recv()
        vectors = [V[base + s, r], V[base + flip, r], V[base + s + 4, r], V[y_next, r],
                   T[img, odd, s, r]]
        blocks = [C[s], F[24 + s], F[8 + s], F[16 + s], F[s]]
        total = times(jnp.concatenate(vectors, axis=1), jnp.concatenate(blocks, axis=1))
        for formed in (PX[img * 8 + flip, r], PZ[img * 12 + s, r], PY[y_from, r],
                       T[img, 1 + odd, s, r]):
            total = total + formed.astype(jnp.float32)
        value = total.astype(jnp.bfloat16)

        if img == 0:
            V[16 + s, r] = value
            form(1, r, s, value)
            send_y(u + 8)
        else:
            O[s, r] = value
            result(q).start()
            total_r[r] += times(value, R[s])

            if s == 7:
                own_r[r] = total_r[r].astype(jnp.bfloat16)
                for copy in gather(q - UNITS + 1):
                    copy.start()

        if u + Z_AHEAD < UNITS:
            send_z(u + Z_AHEAD)

    finished = 0
    for q in range(PIECES + 1):
        if q < PIECES:
            img, r, s = piece(q)
            near(q, V.at[0]).wait_recv()

            if q < 8:
                block0(s).wait_recv()

            T[img, 2, s, r] = times(T[img, 0, s, r], B0[s]).astype(jnp.bfloat16)
            far(q).start()

        if q + AHEAD < PIECES:
            later, _, site = piece(q + AHEAD)
            send_time(q + AHEAD, V.at[later * 16 + site])

        lag = LAG if q < UNITS - 3 else LAG - 1 if q < UNITS else LAG - 2
        ready = q - lag if q < PIECES else PIECES - 1
        while finished <= ready:
            finish(finished)
            finished += 1

    for u in range(UNITS):
        z_any(u).wait_send()
        y_any(u).wait_send()

    for q in range(PIECES):
        near(q, V.at[0]).wait_send()
        far(q).wait_send()

    for s in range(8):
        block0(s).wait_send()

    for q in range(8, PIECES):
        result(q).wait()

    for part in range(2):
        for copy in gather(part):
            copy.wait()


def write(image, gathered, image_out, gathered_out, held, inward, outward):
    parts = [(image.at[s], image_out.at[s]) for s in range(image.shape[0])]
    parts += [(gathered.at[s], gathered_out.at[s]) for s in range(gathered.shape[0])]
    reads = [pltpu.make_async_copy(a, held.at[i], inward.at[i]) for i, (a, _) in enumerate(parts)]
    writes = [pltpu.make_async_copy(held.at[i], b, outward.at[i]) for i, (_, b) in enumerate(parts)]
    for copy in reads:
        copy.start()
    for read, copy in zip(reads, writes):
        read.wait()
        copy.start()
    for copy in writes:
        copy.wait()


def written(image, gathered):
    count = image.shape[0] + gathered.shape[0]
    return pl.pallas_call(
        write,
        out_shape=(
            jax.ShapeDtypeStruct(image.shape, image.dtype),
            jax.ShapeDtypeStruct(gathered.shape, gathered.dtype),
        ),
        in_specs=[pl.BlockSpec(memory_space=pltpu.HBM)] * 2,
        out_specs=(pl.BlockSpec(memory_space=pltpu.HBM), pl.BlockSpec(memory_space=pltpu.HBM)),
        scratch_shapes=[
            pltpu.VMEM((count,) + image.shape[1:], image.dtype),
            pltpu.SemaphoreType.DMA((count,)),
            pltpu.SemaphoreType.DMA((count,)),
        ],
        compiler_params=pltpu.CompilerParams(vmem_limit_bytes=60 * 1024 * 1024),
    )(image, gathered)


def per_device(sizes, source_field, clover, forward, backward, restrict_blocks):
    n_ta, n_gz, n_gy = sizes
    rows, width = source_field.shape[-2:]
    field = (rows, width)
    block = (width, width)
    others = n_gz * n_gy - 1
    bf16 = jnp.bfloat16
    dma = pltpu.SemaphoreType.DMA
    image, gathered = pl.pallas_call(
        functools.partial(kernel, sizes),
        out_shape=(
            jax.ShapeDtypeStruct((8,) + field, bf16),
            jax.ShapeDtypeStruct((n_gz * n_gy,) + field, bf16),
        ),
        in_specs=[pl.BlockSpec(memory_space=pltpu.HBM)] * 5,
        out_specs=(pl.BlockSpec(memory_space=pltpu.HBM), pl.BlockSpec(memory_space=pltpu.HBM)),
        scratch_shapes=[
            pltpu.VMEM((32,) + field, bf16),
            pltpu.VMEM((2, 3, 8) + field, bf16),
            pltpu.VMEM((24,) + field, bf16),
            pltpu.VMEM((24,) + field, bf16),
            pltpu.VMEM((16,) + field, bf16),
            pltpu.VMEM((8,) + block, bf16),
            pltpu.VMEM((8,) + block, bf16),
            pltpu.VMEM((32,) + block, bf16),
            pltpu.VMEM((24,) + block, bf16),
            pltpu.VMEM((8,) + block, bf16),
            pltpu.VMEM((8,) + field, bf16),
            pltpu.VMEM(field, jnp.float32),
            pltpu.VMEM(field, bf16),
            dma((PIECES,)), dma((PIECES,)), dma((PIECES,)), dma((PIECES,)),
            dma((8,)), dma((8,)),
            dma((UNITS,)), dma((UNITS,)), dma((UNITS,)), dma((UNITS,)),
            dma((5,)), dma((PIECES - 8,)), dma((2, others)), dma((2, others)), dma((2,)),
        ],
        compiler_params=pltpu.CompilerParams(
            collective_id=0, has_side_effects=True, vmem_limit_bytes=60 * 1024 * 1024
        ),
    )(
        source_field.reshape((8,) + field),
        clover.reshape((8,) + block),
        forward.reshape((32,) + block),
        backward.reshape((32,) + block),
        restrict_blocks.reshape((8,) + block),
    )
    image, gathered = written(image, gathered)
    return image.reshape(source_field.shape), gathered.reshape((1, n_gz * n_gy) + field)


def solution(mesh):
    sizes = tuple(mesh.shape[axis] for axis in ("ta", "gz", "gy"))
    assert sizes[0] % 2 == 0 and sizes[0] >= 4
    return jax.shard_map(
        functools.partial(per_device, sizes),
        mesh=mesh,
        in_specs=(
            P("ta", "gz", "gy", None, None, None),
            P("ta", "gz", "gy", None, None, None),
            P(None, "ta", "gz", "gy", None, None, None),
            P(None, "ta", "gz", "gy", None, None, None),
            P("ta", "gz", "gy", None, None, None),
        ),
        out_specs=(P("ta", "gz", "gy", None, None, None), P("ta", None, None, None)),
        check_vma=False,
    )
```

```python
import functools

import jax
import jax.numpy as jnp
from jax import lax
from jax.experimental import pallas as pl
from jax.experimental.pallas import tpu as pltpu
from jax.sharding import PartitionSpec as P

MESH = pl.DeviceIdType.MESH
LAG = 4
Z_AHEAD = 4
UNITS = 16
PIECES = 17


def times(vector, block):
    return lax.dot_general(
        vector, block, (((1,), (1,)), ((), ())), preferred_element_type=jnp.float32
    )


def kernel(
    sizes,
    src, clo, fwd, bwd, res,
    image, gathered,
    V, T, PZ, PY, PX, B0, C, F, B, R, O, total_r, own_r,
    near_send, near_recv, far_send, far_recv, b0_send, b0_recv,
    z_send, z_recv, y_send, y_recv, local, out_sem, g_send, g_recv, g_local,
):
    n_ta, n_gz, n_gy = sizes
    ta, gz, gy = lax.axis_index("ta"), lax.axis_index("gz"), lax.axis_index("gy")
    odd = lax.rem(ta, 2)
    partner = ta + 1 - 2 * odd
    beyond = lax.rem(ta + 2 - 4 * odd + n_ta, n_ta)
    z_up, z_down = lax.rem(gz + 1, n_gz), lax.rem(gz + n_gz - 1, n_gz)
    y_up, y_down = lax.rem(gy + 1, n_gy), lax.rem(gy + n_gy - 1, n_gy)

    fetch = [
        pltpu.make_async_copy(src, V.at[pl.ds(0, 8)], local.at[0]),
        pltpu.make_async_copy(bwd.at[pl.ds(8, 24)], B, local.at[1]),
        pltpu.make_async_copy(fwd, F, local.at[2]),
        pltpu.make_async_copy(clo, C, local.at[3]),
        pltpu.make_async_copy(res, R, local.at[4]),
    ]
    for copy in fetch:
        copy.start()

    others = [(a, b) for a in range(n_gz) for b in range(n_gy) if (a, b) != (0, 0)]

    def other(a, b):
        return lax.rem(gz + a, n_gz), lax.rem(gz * 0 + gy + b, n_gy)

    barrier = pltpu.get_barrier_semaphore()
    for neighbour in (partner, lax.rem(ta + 2, n_ta), lax.rem(ta + n_ta - 2, n_ta)):
        pl.semaphore_signal(barrier, inc=1, device_id=(neighbour, gz, gy), device_id_type=MESH)
    for a, b in others:
        oz, oy = other(a, b)
        pl.semaphore_signal(barrier, inc=1, device_id=(ta, oz, oy), device_id_type=MESH)
    pl.semaphore_wait(barrier, 3 + len(others))

    def remote(source, target, send, recv, device):
        return pltpu.make_async_remote_copy(
            src_ref=source, dst_ref=target, send_sem=send, recv_sem=recv,
            device_id=device, device_id_type=MESH,
        )

    rows = src.shape[1]
    half = rows // 2

    def split(u):
        return u // 8, pl.ds(0, rows), u % 8

    def piece(q):
        if q < UNITS - 1:
            return q // 8, pl.ds(0, rows), q % 8
        return 1, pl.ds((q - UNITS + 1) * half, half), 7

    def near(q, source):
        img, r, s = piece(q)
        return remote(source.at[r], T.at[img, 0, s, r], near_send.at[q], near_recv.at[q],
                      (partner, gz, gy))

    def far(q):
        img, r, s = piece(q)
        return remote(T.at[img, 2 - 2 * odd, s, r], T.at[img, 1, s, r], far_send.at[q],
                      far_recv.at[q], (beyond, gz, gy))

    def block0(s):
        return remote(bwd.at[s], B0.at[s], b0_send.at[s], b0_recv.at[s], (partner, gz, gy))

    def z_vector(u):
        img, r, s = split(u)
        return remote(V.at[img * 16 + s, r], V.at[img * 16 + 8 + s, r], z_send.at[u],
                      z_recv.at[u + 4], (ta, z_down, gy))

    def z_formed(u):
        img, r, s = split(u)
        return remote(PZ.at[img * 12 + 4 + s, r], PZ.at[img * 12 + s - 4, r], z_send.at[u],
                      z_recv.at[u - 4], (ta, z_up, gy))

    def z_any(u):
        return remote(V.at[0, pl.ds(0, rows)], V.at[0, pl.ds(0, rows)], z_send.at[u],
                      z_recv.at[u], (ta, z_up, gy))

    def y_vector(u):
        img, r, s = split(u)
        k = 2 * (s // 4) + s % 2
        return remote(V.at[img * 16 + s, r], V.at[img * 16 + 12 + k, r], y_send.at[u],
                      y_recv.at[u + 2], (ta, gz, y_down))

    def y_formed(u):
        img, r, s = split(u)
        k = 2 * (s // 4) + s % 2
        return remote(PY.at[img * 12 + s, r], PY.at[img * 12 + 8 + k, r], y_send.at[u],
                      y_recv.at[u - 2], (ta, gz, y_up))

    def y_any(u):
        return remote(V.at[0, pl.ds(0, rows)], V.at[0, pl.ds(0, rows)], y_send.at[u],
                      y_recv.at[u], (ta, gz, y_up))

    def send_time(u, source):
        if u < 8:
            block0(u % 8).start()

        near(u, source).start()

    def send_z(target):
        if target % 8 < 4:
            z_formed(target + 4).start()

        if target % 8 >= 4:
            z_vector(target - 4).start()

    def send_y(u):
        y = (u // 2) % 2

        if y == 0:
            y_vector(u).start()

        if y == 1:
            y_formed(u).start()

    def form(img, r, s, vector):
        block = jnp.concatenate([B[s], B[8 + s], B[16 + s]], axis=0)
        formed = times(vector, block).astype(jnp.bfloat16)
        width = vector.shape[1]
        PZ[img * 12 + 4 + s, r] = formed[:, :width]
        PY[img * 12 + s, r] = formed[:, width : 2 * width]
        PX[img * 8 + s, r] = formed[:, 2 * width :]

    for u in range(8):
        send_time(u, src.at[u % 8])

    fetch[0].wait()
    fetch[1].wait()

    for index in range(0, 8):
        s = (index + 4) % 8
        everything = pl.ds(0, rows)
        form(0, everything, s, V[s])

        if index < 4:
            send_z(index)

        send_y(s)

    for copy in fetch[2:]:
        copy.wait()
    total_r[...] = jnp.zeros_like(total_r)

    place = gz * n_gy + gy

    def gather(part):
        r = pl.ds(part * half, half)
        copies = [pltpu.make_async_copy(own_r.at[r], gathered.at[place, r], g_local.at[part])]
        for index, (a, b) in enumerate(others):
            oz, oy = other(a, b)
            copies.append(remote(own_r.at[r], gathered.at[place, r], g_send.at[part, index],
                                 g_recv.at[part, index], (ta, oz, oy)))
        return copies

    def result(q):
        img, r, s = piece(q)
        return pltpu.make_async_copy(O.at[s, r], image.at[s, r], out_sem.at[q - 8])

    def finish(q):
        img, r, s = piece(q)
        u = img * 8 + s
        z, y, x = s // 4, (s // 2) % 2, s % 2
        k = 2 * z + x
        base = img * 16
        y_next = base + (1 - y) * (s + 2) + y * (12 + k)
        y_from = img * 12 + y * (s - 2) + (1 - y) * (8 + k)
        flip = s + 1 - 2 * x

        if q == u:
            z_any(u).wait_recv()
            y_any(u).wait_recv()
        far(q).wait_recv()
        vectors = [V[base + s, r], V[base + flip, r], V[base + s + 4, r], V[y_next, r],
                   T[img, odd, s, r]]
        blocks = [C[s], F[24 + s], F[8 + s], F[16 + s], F[s]]
        total = times(jnp.concatenate(vectors, axis=1), jnp.concatenate(blocks, axis=1))
        for formed in (PX[img * 8 + flip, r], PZ[img * 12 + s, r], PY[y_from, r],
                       T[img, 1 + odd, s, r]):
            total = total + formed.astype(jnp.float32)
        value = total.astype(jnp.bfloat16)

        if img == 0:
            V[16 + s, r] = value
            for later in range(u + 8, PIECES if s == 7 else u + 9):
                near(later, V.at[16 + s]).start()
            form(1, r, s, value)
            send_y(u + 8)
        else:
            O[s, r] = value
            result(q).start()
            total_r[r] += times(value, R[s])

            if s == 7:
                own_r[r] = total_r[r].astype(jnp.bfloat16)
                for copy in gather(q - UNITS + 1):
                    copy.start()

        if u + Z_AHEAD < UNITS:
            send_z(u + Z_AHEAD)

    finished = 0
    for q in range(PIECES + 1):
        if q < PIECES:
            img, r, s = piece(q)
            near(q, V.at[0]).wait_recv()

            if q < 8:
                block0(s).wait_recv()

            T[img, 2, s, r] = times(T[img, 0, s, r], B0[s]).astype(jnp.bfloat16)
            far(q).start()

        lag = LAG if q < UNITS - 3 else LAG - 1 if q < UNITS else LAG - 2
        ready = q - lag if q < PIECES else PIECES - 1
        while finished <= ready:
            finish(finished)
            finished += 1

    for u in range(UNITS):
        z_any(u).wait_send()
        y_any(u).wait_send()

    for q in range(PIECES):
        near(q, V.at[0]).wait_send()
        far(q).wait_send()

    for s in range(8):
        block0(s).wait_send()

    for q in range(8, PIECES):
        result(q).wait()

    for part in range(2):
        for copy in gather(part):
            copy.wait()


def write(image, gathered, image_out, gathered_out, held, inward, outward):
    parts = [(image.at[s], image_out.at[s]) for s in range(image.shape[0])]
    parts += [(gathered.at[s], gathered_out.at[s]) for s in range(gathered.shape[0])]
    reads = [pltpu.make_async_copy(a, held.at[i], inward.at[i]) for i, (a, _) in enumerate(parts)]
    writes = [pltpu.make_async_copy(held.at[i], b, outward.at[i]) for i, (_, b) in enumerate(parts)]
    for copy in reads:
        copy.start()
    for read, copy in zip(reads, writes):
        read.wait()
        copy.start()
    for copy in writes:
        copy.wait()


def written(image, gathered):
    count = image.shape[0] + gathered.shape[0]
    return pl.pallas_call(
        write,
        out_shape=(
            jax.ShapeDtypeStruct(image.shape, image.dtype),
            jax.ShapeDtypeStruct(gathered.shape, gathered.dtype),
        ),
        in_specs=[pl.BlockSpec(memory_space=pltpu.HBM)] * 2,
        out_specs=(pl.BlockSpec(memory_space=pltpu.HBM), pl.BlockSpec(memory_space=pltpu.HBM)),
        scratch_shapes=[
            pltpu.VMEM((count,) + image.shape[1:], image.dtype),
            pltpu.SemaphoreType.DMA((count,)),
            pltpu.SemaphoreType.DMA((count,)),
        ],
        compiler_params=pltpu.CompilerParams(vmem_limit_bytes=60 * 1024 * 1024),
    )(image, gathered)


def per_device(sizes, source_field, clover, forward, backward, restrict_blocks):
    n_ta, n_gz, n_gy = sizes
    rows, width = source_field.shape[-2:]
    field = (rows, width)
    block = (width, width)
    others = n_gz * n_gy - 1
    bf16 = jnp.bfloat16
    dma = pltpu.SemaphoreType.DMA
    image, gathered = pl.pallas_call(
        functools.partial(kernel, sizes),
        out_shape=(
            jax.ShapeDtypeStruct((8,) + field, bf16),
            jax.ShapeDtypeStruct((n_gz * n_gy,) + field, bf16),
        ),
        in_specs=[pl.BlockSpec(memory_space=pltpu.HBM)] * 5,
        out_specs=(pl.BlockSpec(memory_space=pltpu.HBM), pl.BlockSpec(memory_space=pltpu.HBM)),
        scratch_shapes=[
            pltpu.VMEM((32,) + field, bf16),
            pltpu.VMEM((2, 3, 8) + field, bf16),
            pltpu.VMEM((24,) + field, bf16),
            pltpu.VMEM((24,) + field, bf16),
            pltpu.VMEM((16,) + field, bf16),
            pltpu.VMEM((8,) + block, bf16),
            pltpu.VMEM((8,) + block, bf16),
            pltpu.VMEM((32,) + block, bf16),
            pltpu.VMEM((24,) + block, bf16),
            pltpu.VMEM((8,) + block, bf16),
            pltpu.VMEM((8,) + field, bf16),
            pltpu.VMEM(field, jnp.float32),
            pltpu.VMEM(field, bf16),
            dma((PIECES,)), dma((PIECES,)), dma((PIECES,)), dma((PIECES,)),
            dma((8,)), dma((8,)),
            dma((UNITS,)), dma((UNITS,)), dma((UNITS,)), dma((UNITS,)),
            dma((5,)), dma((PIECES - 8,)), dma((2, others)), dma((2, others)), dma((2,)),
        ],
        compiler_params=pltpu.CompilerParams(
            collective_id=0, has_side_effects=True, vmem_limit_bytes=60 * 1024 * 1024
        ),
    )(
        source_field.reshape((8,) + field),
        clover.reshape((8,) + block),
        forward.reshape((32,) + block),
        backward.reshape((32,) + block),
        restrict_blocks.reshape((8,) + block),
    )
    image, gathered = written(image, gathered)
    return image.reshape(source_field.shape), gathered.reshape((1, n_gz * n_gy) + field)


def solution(mesh):
    sizes = tuple(mesh.shape[axis] for axis in ("ta", "gz", "gy"))
    assert sizes[0] % 2 == 0 and sizes[0] >= 4
    return jax.shard_map(
        functools.partial(per_device, sizes),
        mesh=mesh,
        in_specs=(
            P("ta", "gz", "gy", None, None, None),
            P("ta", "gz", "gy", None, None, None),
            P(None, "ta", "gz", "gy", None, None, None),
            P(None, "ta", "gz", "gy", None, None, None),
            P("ta", "gz", "gy", None, None, None),
        ),
        out_specs=(P("ta", "gz", "gy", None, None, None), P("ta", None, None, None)),
        check_vma=False,
    )
```
